256 devices in a mesh: dp: 4 (over x), pool: 16 (over z, core), head: 4 (over y).
Axes of the slice: x: 4, y: 4, z: 8, core: 2. Of those that a mesh axis runs over, the one named last changes fastest.
Arguments:
- x_prompt: bfloat16 [4, 1024, 4096], P('dp', 'pool'), may hold values from -6 to 6
- x_resp: bfloat16 [4, 4096, 4096], P('dp', 'pool'), may hold values from -6 to 6
- w_kv: bfloat16 [4096, 1024], P(None, 'head'), may hold values from -0.09375 to 0.09375
- q_prompt: bfloat16 [4, 1024, 8192], P('dp', 'pool', 'head'), may hold values from -5 to 5
- q_resp: bfloat16 [4, 4096, 8192], P('dp', 'pool', 'head'), may hold values from -5 to 5
- do_prompt: bfloat16 [4, 1024, 8192], P('dp', 'pool', 'head'), may hold values from -6 to 6
- do_resp: bfloat16 [4, 4096, 8192], P('dp', 'pool', 'head'), may hold values from -6 to 6
- resp_len: int32 [4, 16], P('dp', 'pool'), may hold values from 64 to 256, as said below
Outputs:
- attn_prompt: bfloat16 [4, 1024, 8192], P('dp', 'pool', 'head')
- attn_resp: bfloat16 [4, 4096, 8192], P('dp', 'pool', 'head')
- grad_q_prompt: bfloat16 [4, 1024, 8192], P('dp', 'pool', 'head')
- grad_q_resp: bfloat16 [4, 4096, 8192], P('dp', 'pool', 'head')
- grad_x_prompt: bfloat16 [4, 1024, 4096], P('dp', 'pool', 'head')
- grad_x_resp: bfloat16 [4, 4096, 4096], P('dp', 'pool', 'head')
- grad_w_kv: float32 [4096, 1024], P(('dp', 'pool'), 'head')
The draws below stay inside these ranges and needn't reach their ends.
Inputs may be any that keep to these rules, and one draw needn't show every extreme that they name: `resp_len`: at least one response in every draw has all 256 tokens live.
All inputs are finite; a program needn't handle non-finite values.
Results may differ from the reference program's by a relative error of at most 0.029.
Values may be sent and summed in bfloat16 or wider, within the bound.
A program may use at most 64 MiB of HBM per device.

```python
import math
import jax
import jax.numpy as jnp
from jax import lax

D = 4096
QH = 64
KV_HEADS = 4
HEAD_DIM = 128
PROMPT_DEV = 64
RESP_DEV = 256
PROMPT_LEN = 1024
RESP_TOKENS = 4096
N_DP = 4
N_POOL = 16


def draw_resp_len(key, part):
    key = jax.random.fold_in(key, 5)
    first, second = jax.random.split(key)
    lengths = jax.random.randint(first, (N_DP * N_POOL,), RESP_DEV // 4, RESP_DEV + 1)
    spot = jax.random.randint(second, (), 0, N_DP * N_POOL)
    lengths = jnp.where(jnp.arange(N_DP * N_POOL) == spot, RESP_DEV, lengths)
    return lengths.reshape(N_DP, N_POOL).astype(jnp.int32)


def spiked(array, key, source, target, blocks, factor):
    owner, partner = [(jnp.arange(array.shape[axis_at]) // (array.shape[axis_at] // blocks)).reshape([-1 if axis == axis_at else 1 for axis in range(array.ndim)]) for axis_at in (source, target)]
    chosen = jax.random.permutation(key, blocks)[partner]
    strong = (owner == chosen) | (owner == (partner + blocks // 2) % blocks)
    return jnp.where(strong, factor * array, array)


def steps_of(rng, shape, cuts, smallest, largest):
    factor_of = 1.0
    for dim, blocks in cuts:
        draws = jax.random.uniform(jax.random.fold_in(jax.random.fold_in(rng, 6), dim), (blocks,), jnp.float32, smallest / len(cuts), largest / len(cuts))
        factor_of = factor_of * jnp.repeat(jnp.exp(draws), shape[dim] // blocks).reshape((-1,) + (1,) * (len(shape) - 1 - dim))
    return factor_of


def bell_draw(stream_key, extent, spread, limit, shards=(), dtype=jnp.bfloat16):
    drawn = spread * jax.random.normal(stream_key, extent, jnp.float32)
    if shards:
        drawn = drawn * steps_of(stream_key, extent, shards, -0.22, 0.18)
    return jnp.clip(drawn, -limit, limit).astype(dtype)


def gaussian_with(key, extent, scale, bound, shards, heavy, dtype=jnp.bfloat16):
    array = scale * jax.random.normal(key, extent, jnp.float32)
    if shards:
        array = array * steps_of(key, extent, shards, -0.22, 0.18)
    return jnp.clip(spiked(array, jax.random.fold_in(key, 3), *heavy), -bound, bound).astype(dtype)


def setup_inputs(seed: int = 0) -> dict:
    splits = jax.random.split(jax.random.key(seed), 9)
    x_prompt = bell_draw(splits[0], (N_DP, PROMPT_LEN, D), 1.0, 6.0, ((0, 4), (1, 16)))
    x_resp = gaussian_with(splits[1], (N_DP, RESP_TOKENS, D), 1.0, 6.0, ((0, 4), (1, 16)), (1, 2, 16, 2.0))
    w_kv = bell_draw(splits[2], (D, KV_HEADS * 2 * HEAD_DIM), D ** -0.5, 0.09375, ((1, 4),))
    q_prompt = bell_draw(splits[3], (N_DP, PROMPT_LEN, QH * HEAD_DIM), 1.0, 5.0, ((0, 4), (1, 16), (2, 4)))
    q_resp = bell_draw(splits[4], (N_DP, RESP_TOKENS, QH * HEAD_DIM), 1.0, 5.0, ((0, 4), (1, 16), (2, 4)))
    do_prompt = bell_draw(splits[5], (N_DP, PROMPT_LEN, QH * HEAD_DIM), 1.0, 6.0, ((0, 4), (1, 16), (2, 4)))
    do_resp = bell_draw(splits[6], (N_DP, RESP_TOKENS, QH * HEAD_DIM), 1.0, 6.0, ((0, 4), (1, 16), (2, 4)))
    resp_len = draw_resp_len(jax.random.fold_in(splits[8], 71), 0)
    return {"x_prompt": x_prompt, "x_resp": x_resp, "w_kv": w_kv, "q_prompt": q_prompt, "q_resp": q_resp, "do_prompt": do_prompt, "do_resp": do_resp, "resp_len": resp_len}


def core(query, grad_out, keys, values, allowed):
    scale = 1.0 / math.sqrt(query.shape[-1])
    scores = jnp.dot(query, keys.T, preferred_element_type=jnp.float32) * scale
    expo = jnp.where(allowed, jnp.exp(scores), 0.0)
    weights = expo / lax.optimization_barrier(jnp.sum(expo, axis=-1, keepdims=True))
    rounded = weights.astype(jnp.bfloat16)
    output = jnp.dot(rounded, values, preferred_element_type=jnp.float32).astype(jnp.bfloat16)
    grad_weights = jnp.dot(grad_out, values.T, preferred_element_type=jnp.float32)
    delta = lax.optimization_barrier(jnp.sum(grad_out.astype(jnp.float32) * output.astype(jnp.float32), axis=-1, keepdims=True))
    grad_scores = (weights * (grad_weights - delta)).astype(jnp.bfloat16)
    grad_query = (jnp.dot(grad_scores, keys, preferred_element_type=jnp.float32) * scale).astype(jnp.bfloat16)
    grad_keys = jnp.dot(grad_scores.T, query, preferred_element_type=jnp.float32) * scale
    grad_values = jnp.dot(rounded.T, grad_out, preferred_element_type=jnp.float32)
    return (output, grad_query, grad_keys, grad_values)

def reference(x_prompt, x_resp, w_kv, q_prompt, q_resp, do_prompt, do_resp, resp_len):
    group = QH // KV_HEADS
    width = 2 * HEAD_DIM
    prompt_total = PROMPT_DEV * N_POOL
    resp_total = RESP_DEV * N_POOL
    w_heads = w_kv.reshape(D, KV_HEADS, width).transpose(1, 0, 2)
    prompt_allowed = jnp.arange(prompt_total)[None, :] <= jnp.arange(prompt_total)[:, None]
    row_ids = jnp.arange(RESP_DEV)[:, None]
    col_ids = jnp.arange(prompt_total + RESP_DEV)[None, :] - prompt_total

    def one_group(inputs):
        hid_prompt, hid_resp, qp_all, qr_all, dop_all, dor_all, lengths = inputs
        valid = jnp.arange(RESP_DEV)[None, :] < lengths[:, None]
        dor_rows = dor_all.reshape(N_POOL, RESP_DEV, QH * HEAD_DIM)
        dor_rows = jnp.where(valid[:, :, None], dor_rows, jnp.zeros_like(dor_rows))
        qp_heads = qp_all.reshape(prompt_total, KV_HEADS, group, HEAD_DIM).transpose(1, 2, 0, 3)
        dop_heads = dop_all.reshape(prompt_total, KV_HEADS, group, HEAD_DIM).transpose(1, 2, 0, 3)
        qr_heads = qr_all.reshape(N_POOL, RESP_DEV, KV_HEADS, group, HEAD_DIM).transpose(2, 3, 0, 1, 4)
        dor_heads = dor_rows.reshape(N_POOL, RESP_DEV, KV_HEADS, group, HEAD_DIM).transpose(2, 3, 0, 1, 4)

        def kv_head(carry, items):
            dx_prompt, dx_resp = carry
            w_head, qph, doph, qrh, dorh = items
            kv_p = jnp.dot(hid_prompt, w_head, preferred_element_type=jnp.float32).astype(jnp.bfloat16)
            kv_r = jnp.dot(hid_resp, w_head, preferred_element_type=jnp.float32).astype(jnp.bfloat16)
            kv_r = kv_r.reshape(N_POOL, RESP_DEV, width)
            keys_p = kv_p[:, :HEAD_DIM]
            values_p = kv_p[:, HEAD_DIM:]

            def resp_one(query, grad_out, kv_one, length):
                keys = jnp.concatenate([keys_p, kv_one[:, :HEAD_DIM]], axis=0)
                values = jnp.concatenate([values_p, kv_one[:, HEAD_DIM:]], axis=0)
                allowed = (col_ids < 0) | (col_ids <= row_ids) & (col_ids < length)
                return core(query, grad_out, keys, values, allowed)

            def q_head(acc, parts):
                grad_p, grad_r = acc
                qp, dop, qr, dor = parts
                out_p, dq_p, dk_p, dv_p = core(qp, dop, keys_p, values_p, prompt_allowed)
                out_r, dq_r, dk_a, dv_a = jax.vmap(resp_one)(qr, dor, kv_r, lengths)
                grad_p = grad_p + jnp.concatenate([dk_p + lax.optimization_barrier(jnp.sum(dk_a[:, :prompt_total], axis=0)), dv_p + lax.optimization_barrier(jnp.sum(dv_a[:, :prompt_total], axis=0))], axis=1)
                grad_r = grad_r + jnp.concatenate([dk_a[:, prompt_total:], dv_a[:, prompt_total:]], axis=2)
                return ((grad_p, grad_r), (out_p, out_r, dq_p, dq_r))
            start = (jnp.zeros((prompt_total, width), jnp.float32), jnp.zeros((N_POOL, RESP_DEV, width), jnp.float32))
            (grad_p, grad_r), outs = lax.scan(q_head, start, (qph, doph, qrh, dorh))
            grad_pb = grad_p.astype(jnp.bfloat16)
            grad_rb = grad_r.reshape(resp_total, width).astype(jnp.bfloat16)
            grad_w = jnp.dot(hid_prompt.T, grad_pb, preferred_element_type=jnp.float32) + jnp.dot(hid_resp.T, grad_rb, preferred_element_type=jnp.float32)
            term_p = lax.optimization_barrier(jnp.dot(grad_pb, w_head.T, preferred_element_type=jnp.float32).astype(jnp.bfloat16))
            term_r = lax.optimization_barrier(jnp.dot(grad_rb, w_head.T, preferred_element_type=jnp.float32).astype(jnp.bfloat16))
            return ((dx_prompt + term_p.astype(jnp.float32), dx_resp + term_r.astype(jnp.float32)), (grad_w,) + outs)
        start = (jnp.zeros((prompt_total, D), jnp.float32), jnp.zeros((resp_total, D), jnp.float32))
        (dx_prompt, dx_resp), stacked = lax.scan(kv_head, start, (w_heads, qp_heads, dop_heads, qr_heads, dor_heads))
        grad_w, out_p, out_r, dq_p, dq_r = stacked
        attn_p = out_p.transpose(2, 0, 1, 3).reshape(prompt_total, QH * HEAD_DIM)
        attn_r = out_r.transpose(2, 3, 0, 1, 4).reshape(resp_total, QH * HEAD_DIM)
        gq_p = dq_p.transpose(2, 0, 1, 3).reshape(prompt_total, QH * HEAD_DIM)
        gq_r = dq_r.transpose(2, 3, 0, 1, 4).reshape(resp_total, QH * HEAD_DIM)
        return (attn_p, attn_r, gq_p, gq_r, dx_prompt.astype(jnp.bfloat16), dx_resp.astype(jnp.bfloat16), grad_w)
    results = lax.map(one_group, (x_prompt, x_resp, q_prompt, q_resp, do_prompt, do_resp, resp_len))
    attn_p, attn_r, gq_p, gq_r, gx_p, gx_r, grad_w = results
    grad_w_kv = lax.optimization_barrier(jnp.sum(grad_w, axis=0)).transpose(1, 0, 2).reshape(D, KV_HEADS * width)
    return (attn_p, attn_r, gq_p, gq_r, gx_p, gx_r, grad_w_kv)
```

```python
import math

import jax
import jax.numpy as jnp
from jax import lax
from jax.experimental import pallas as pl
from jax.experimental.pallas import tpu as pltpu
from jax.sharding import PartitionSpec as P

HD = 128
LN2 = math.log(2.0)
SCALE = 1.0 / math.sqrt(HD)
KFOLD = SCALE / LN2
F32 = jnp.float32
BF = jnp.bfloat16
MESH = pl.DeviceIdType.MESH
CH = 256
VMEM = pl.BlockSpec(memory_space=pltpu.VMEM)


def dot(a, b):
    return jnp.dot(a, b, preferred_element_type=F32)


def dot_nt(a, b):
    return lax.dot_general(a, b, (((1,), (1,)), ((), ())), preferred_element_type=F32)


def dot_tn(a, b):
    return lax.dot_general(a, b, (((0,), (0,)), ((), ())), preferred_element_type=F32)


def remote(src, dst, send, recv, device):
    return pltpu.make_async_remote_copy(
        src_ref=src, dst_ref=dst, send_sem=send, recv_sem=recv,
        device_id=device, device_id_type=MESH,
    )


def greet(devices):
    barrier = pltpu.get_barrier_semaphore()
    for device in devices:
        pl.semaphore_signal(barrier, inc=1, device_id=device, device_id_type=MESH)
    pl.semaphore_wait(barrier, len(devices))


FAR = (4, 3, 5, 2, 6, 1, 7)
NEAR = (1, 7, 2, 6, 3, 5, 4)


def position():
    d, p, h = lax.axis_index("dp"), lax.axis_index("pool"), lax.axis_index("head")
    return d, p // 2, p % 2, h


def project_kernel(xp, xr, w, kv, send, recv, fsend, frecv):
    d, z, c, h = position()
    at = lambda zz, cc: (d, lax.rem(zz, 8) * 2 + cc, h)
    greet([at(z + k, c) for k in range(1, 8)] + [at(z, 1 - c)])
    lane = lax.broadcasted_iota(jnp.int32, (1, 2 * HD), 1)
    fold = jnp.where(lane < HD, KFOLD, 1.0).astype(F32)
    mine = z * 2 + c
    kv[mine] = (dot(xp[...], w[...]) * fold).astype(BF)
    copies = []
    for k in FAR:
        copy = remote(kv.at[mine], kv.at[mine], send.at[k], recv.at[k], at(z + k, c))
        copy.start()
        copies.append(copy)
    pair = remote(kv.at[mine], kv.at[mine], send.at[0], recv.at[0], at(z, 1 - c))
    pair.start()
    for i in range(4):
        kv[16 + i] = (dot(xr[i * 64:(i + 1) * 64, :], w[...]) * fold).astype(BF)
    forwards = []
    for k in NEAR:
        came = lax.rem(z + 8 - k, 8) * 2 + c
        remote(kv.at[came], kv.at[came], send.at[k], recv.at[k], at(z + k, c)).wait_recv()
        copy = remote(kv.at[came], kv.at[came], fsend.at[k], frecv.at[k], at(z, 1 - c))
        copy.start()
        forwards.append(copy)
    pair.wait()
    for copy in copies:
        copy.wait_send()
    for copy in forwards:
        copy.wait()


def project(xp, xr, w):
    return pl.pallas_call(
        project_kernel,
        in_specs=[VMEM] * 3,
        out_specs=VMEM,
        out_shape=jax.ShapeDtypeStruct((20, 64, 256), BF),
        scratch_shapes=[pltpu.SemaphoreType.DMA((8,))] * 4,
        compiler_params=pltpu.CompilerParams(
            collective_id=0, has_side_effects=True, vmem_limit_bytes=40 << 20
        ),
        cost_estimate=pl.CostEstimate(flops=700_000_000, bytes_accessed=5 << 20, transcendentals=0),
        name="project_gather",
    )(xp, xr, w)


def attend(q, do, kv, acc, e_ref, chunks, mask_of):
    rows = q.shape[0]
    total = jnp.zeros((rows, 128), F32)
    for j in range(chunks):
        at = pl.ds(j * CH, CH)
        e = jnp.exp2(dot_nt(q, kv[at, 0:HD]))
        mask = mask_of(j)
        if mask is not None:
            e = jnp.where(mask, e, 0.0)
        e_ref[:, at] = e
        total = total + e[:, :128] + e[:, 128:]
    inverse = 1.0 / jnp.sum(total, axis=1, keepdims=True)
    out = jnp.zeros((rows, HD), F32)
    for j in range(chunks):
        at = pl.ds(j * CH, CH)
        weights = e_ref[:, at] * inverse
        e_ref[:, at] = weights
        out = out + dot(weights.astype(BF), kv[at, HD:])
    out = out.astype(BF)
    delta = jnp.sum(do.astype(F32) * out.astype(F32), axis=1, keepdims=True)
    grad_q = jnp.zeros((rows, HD), F32)
    for j in range(chunks):
        at = pl.ds(j * CH, CH)
        weights = e_ref[:, at]
        grad_s = (weights * (dot_nt(do, kv[at, HD:]) - delta)).astype(BF)
        grad_q = grad_q + dot(grad_s, kv[at, 0:HD])
        acc[0:HD, at] += dot_tn(q, grad_s)
        acc[HD:, at] += dot_tn(do, weights.astype(BF))
    return out, (grad_q * LN2).astype(BF)


def attention_kernel(scalars, qp, dop, qr, dor, kv, op, gqp, out_r, gqr, dkvp, dkvr, acc, e_ref):
    step = pl.program_id(0)
    length, offset = scalars[0], scalars[1]

    @pl.when(step == 0)
    def _():
        acc[...] = jnp.zeros_like(acc)

    def resp_mask(j):
        if j < 4:
            return None
        row = lax.broadcasted_iota(jnp.int32, (256, CH), 0)
        col = lax.broadcasted_iota(jnp.int32, (256, CH), 1)
        return (col <= row) & (col < length)

    def prompt_mask(j):
        row = lax.broadcasted_iota(jnp.int32, (256, CH), 0) % 64
        col = lax.broadcasted_iota(jnp.int32, (256, CH), 1)
        return col + j * CH <= row + offset

    valid = lax.broadcasted_iota(jnp.int32, (256, HD), 0) < length
    for i in range(4):
        head = slice(i * HD, (i + 1) * HD)
        do = dor[:, head]
        do = jnp.where(valid, do, jnp.zeros_like(do))
        out, grad_q = attend(qr[:, head], do, kv, acc, e_ref, 5, resp_mask)
        out_r[:, head] = out
        gqr[:, head] = grad_q
    q = jnp.concatenate([qp[:, i * HD:(i + 1) * HD] for i in range(4)], axis=0)
    do = jnp.concatenate([dop[:, i * HD:(i + 1) * HD] for i in range(4)], axis=0)
    out, grad_q = attend(q, do, kv, acc, e_ref, 4, prompt_mask)
    for i in range(4):
        op[:, i * HD:(i + 1) * HD] = out[i * 64:(i + 1) * 64]
        gqp[:, i * HD:(i + 1) * HD] = grad_q[i * 64:(i + 1) * 64]

    @pl.when(step == 3)
    def _():
        for j in range(10):
            part = acc[:, pl.ds(j * 128, 128)]
            part = jnp.concatenate([part[:HD] * SCALE, part[HD:]], axis=0).T.astype(BF)
            if j < 8:
                dkvp[0, j] = part[:64]
                dkvp[1, j] = part[64:]
            else:
                dkvr[pl.ds((j - 8) * 128, 128), :] = part


def attention(scalars, qp, dop, qr, dor, kv):
    small = pl.BlockSpec((64, 512), lambda g: (0, g))
    large = pl.BlockSpec((256, 512), lambda g: (0, g))
    return pl.pallas_call(
        attention_kernel,
        grid=(4,),
        in_specs=[
            pl.BlockSpec(memory_space=pltpu.SMEM), small, small, large, large,
            pl.BlockSpec((1280, 256), lambda g: (0, 0)),
        ],
        out_specs=[
            small, small, large, large,
            pl.BlockSpec((2, 8, 64, 256), lambda g: (0, 0, 0, 0)),
            pl.BlockSpec((256, 256), lambda g: (0, 0)),
        ],
        out_shape=[jax.ShapeDtypeStruct((64, 2048), BF)] * 2
        + [jax.ShapeDtypeStruct((256, 2048), BF)] * 2
        + [jax.ShapeDtypeStruct((2, 8, 64, 256), BF), jax.ShapeDtypeStruct((256, 256), BF)],
        scratch_shapes=[pltpu.VMEM((256, 1280), F32), pltpu.VMEM((256, 1280), F32)],
        compiler_params=pltpu.CompilerParams(vmem_limit_bytes=40 << 20),
        cost_estimate=pl.CostEstimate(
            flops=20_000_000_000, bytes_accessed=8 << 20, transcendentals=6_500_000
        ),
        name="attend",
    )(scalars, qp, dop, qr, dor, kv)


def total_of(*parts):
    out = parts[0].astype(F32)
    for part in parts[1:]:
        out = out + part.astype(F32)
    return out


def reduce_kernel(
    xp, xr, dkvp, dkvr, w0, w1, w2, w3, gxp, gxr, gw,
    pair_r, t_s, t_r, own, g_r, g_p, lw, pbuf, prcv, x_s, x_r, z_f, z_s, z_r,
    one_s, one_r, t_ss, t_rs, y_ss, y_rs, yp_ss, yp_rs, p_ss, p_rs, x_ss, x_rs, z_ss, z_rs,
):
    d, z, c, h = position()
    s = 1 - 2 * c
    p = z * 2 + c
    at_z = lambda k: (d, lax.rem(z + k, 8) * 2 + c, h)
    at_x = lambda k: (lax.rem(d + 4 + k, 4), p, h)
    at_y = lambda k: (d, p, lax.rem(h + k, 4))
    sibling = (d, z * 2 + 1 - c, h)
    greet(
        [sibling] + [at_z(k) for k in range(1, 8)] + [at_x(1), at_x(-1)] + [at_y(k) for k in range(1, 4)]
    )
    started = []

    def send(*args):
        copy = remote(*args)
        copy.start()
        started.append(copy)
        return copy

    pair = send(dkvp.at[1 - c], pair_r, one_s.at[0], one_r.at[0], sibling)
    heads = [send(dkvr, g_r.at[k], y_ss.at[k], y_rs.at[k], at_y(k)) for k in (1, 2, 3)]
    pair.wait_recv()
    for b in range(8):
        t_s[b] = total_of(dkvp[c, b], pair_r[b]).astype(BF)
    scatter = []
    for k in FAR:
        to = lax.rem(z + k, 8)
        scatter.append(send(t_s.at[to], t_r.at[k], t_ss.at[k], t_rs.at[k], at_z(k)))
    order = (2, 1, 3, 0)
    for i, r in enumerate(order):
        cols = pl.ds(pl.multiple_of(lax.rem(d + r, 4) * 1024, 1024), 1024)
        lw[i] = dot_tn(xr[:, cols], dkvr[...])
    for copy in scatter:
        copy.wait_recv()
    own[...] = total_of(t_s[z], *[t_r[k] for k in range(1, 8)]).astype(BF)
    owners = [send(own, g_p.at[k], yp_ss.at[k], yp_rs.at[k], at_y(k)) for k in (1, 2, 3)]
    halves = []
    for i, r in enumerate(order):
        cols = pl.ds(pl.multiple_of(lax.rem(d + r, 4) * 1024, 1024), 1024)
        piece = (lw[i] + dot_tn(xp[:, cols], own[...])).astype(BF)
        for b in range(16):
            pbuf[i, b % 2, b // 2] = piece[b * 64:(b + 1) * 64]
        halves.append(send(pbuf.at[i, 1 - c], prcv.at[i], p_ss.at[i], p_rs.at[i], sibling))

    def arrived(i):
        remote(pbuf.at[i, 1 - c], prcv.at[i], p_ss.at[i], p_rs.at[i], sibling).wait_recv()

    direct, summed = 2 - c, 1 + c
    arrived(0)
    x_s[0] = total_of(pbuf[0, c], prcv[0]).astype(BF)
    relay = send(x_s.at[0], x_r.at[0], x_ss.at[0], x_rs.at[0], at_x(s))
    arrived(direct)
    x_s[1] = total_of(pbuf[direct, c], prcv[direct]).astype(BF)
    straight = send(x_s.at[1], x_r.at[1], x_ss.at[1], x_rs.at[1], at_x(-s))
    arrived(summed)
    relay.wait_recv()
    x_s[2] = total_of(pbuf[summed, c], prcv[summed], x_r[0]).astype(BF)
    last = send(x_s.at[2], x_r.at[2], x_ss.at[2], x_rs.at[2], at_x(s))
    for copy in heads:
        copy.wait_recv()
    gxr[...] = (
        dot_nt(dkvr[...], w0[...]) + dot_nt(g_r[1], w1[...]) + dot_nt(g_r[2], w2[...]) + dot_nt(g_r[3], w3[...])
    ).astype(BF)
    arrived(3)
    straight.wait_recv()
    last.wait_recv()
    z_f[...] = total_of(pbuf[3, c], prcv[3], x_r[1], x_r[2])
    z_s[...] = z_f[...].astype(BF)
    final = []
    for k in FAR:
        to = lax.rem(z + k, 8)
        final.append(send(z_s.at[to], z_r.at[k], z_ss.at[k], z_rs.at[k], at_z(k)))
    for copy in owners:
        copy.wait_recv()
    gxp[...] = (
        dot_nt(own[...], w0[...]) + dot_nt(g_p[1], w1[...]) + dot_nt(g_p[2], w2[...]) + dot_nt(g_p[3], w3[...])
    ).astype(BF)
    for copy in final:
        copy.wait_recv()
    gw[...] = total_of(z_f[z], *[z_r[k] for k in range(1, 8)])
    for copy in started:
        copy.wait_send()


def reduce(xp, xr, dkvp, dkvr, ws):
    dma = pltpu.SemaphoreType.DMA
    block = (8, 64, 256)
    return pl.pallas_call(
        reduce_kernel,
        in_specs=[VMEM] * 8,
        out_specs=[VMEM] * 3,
        out_shape=[
            jax.ShapeDtypeStruct((64, 1024), BF),
            jax.ShapeDtypeStruct((256, 1024), BF),
            jax.ShapeDtypeStruct((64, 256), F32),
        ],
        scratch_shapes=[
            pltpu.VMEM(block, BF), pltpu.VMEM(block, BF), pltpu.VMEM(block, BF),
            pltpu.VMEM((64, 256), BF), pltpu.VMEM((4, 256, 256), BF), pltpu.VMEM((4, 64, 256), BF),
            pltpu.VMEM((4, 1024, 256), F32), pltpu.VMEM((4, 2) + block, BF), pltpu.VMEM((4,) + block, BF),
            pltpu.VMEM((3,) + block, BF), pltpu.VMEM((3,) + block, BF),
            pltpu.VMEM(block, F32), pltpu.VMEM(block, BF), pltpu.VMEM(block, BF),
            dma((1,)), dma((1,)), dma((8,)), dma((8,)), dma((4,)), dma((4,)), dma((4,)), dma((4,)),
            dma((4,)), dma((4,)), dma((3,)), dma((3,)), dma((8,)), dma((8,)),
        ],
        compiler_params=pltpu.CompilerParams(
            collective_id=1, has_side_effects=True, vmem_limit_bytes=48 << 20
        ),
        cost_estimate=pl.CostEstimate(flops=1_400_000_000, bytes_accessed=7 << 20, transcendentals=0),
        name="reduce_grads",
    )(xp, xr, dkvp, dkvr, *ws)


def body(x_prompt, x_resp, w_kv, q_prompt, q_resp, do_prompt, do_resp, resp_len):
    h = lax.axis_index("head")
    quarter = lambda k: lax.dynamic_slice(w_kv, (lax.rem(h + k, 4) * 1024, 0), (1024, 256))
    ws = [quarter(0)] + [
        lax.ppermute(quarter(k), "head", [(i, (i + k) % 4) for i in range(4)]) for k in (1, 2, 3)
    ]
    kv = project(x_prompt[0], x_resp[0], w_kv).reshape(1280, 256)
    scalars = jnp.stack([resp_len[0, 0], lax.axis_index("pool") * 64]).astype(jnp.int32)
    op, gqp, out_r, gqr, dkvp, dkvr = attention(
        scalars, q_prompt[0], do_prompt[0], q_resp[0], do_resp[0], kv
    )
    gxp, gxr, gw = reduce(x_prompt[0], x_resp[0], dkvp, dkvr, ws)
    return op[None], out_r[None], gqp[None], gqr[None], gxp[None], gxr[None], gw


def solution(mesh):
    return jax.shard_map(
        body,
        mesh=mesh,
        in_specs=(
            P("dp", "pool", None),
            P("dp", "pool", None),
            P(None, "head"),
            P("dp", "pool", "head"),
            P("dp", "pool", "head"),
            P("dp", "pool", "head"),
            P("dp", "pool", "head"),
            P("dp", "pool"),
        ),
        out_specs=(
            P("dp", "pool", "head"),
            P("dp", "pool", "head"),
            P("dp", "pool", "head"),
            P("dp", "pool", "head"),
            P("dp", "pool", "head"),
            P("dp", "pool", "head"),
            P(("dp", "pool"), "head"),
        ),
        check_vma=False,
    )
```

```python
import math

import jax
import jax.numpy as jnp
from jax import lax
from jax.experimental import pallas as pl
from jax.experimental.pallas import tpu as pltpu
from jax.sharding import PartitionSpec as P

HD = 128
LN2 = math.log(2.0)
SCALE = 1.0 / math.sqrt(HD)
KFOLD = SCALE / LN2
F32 = jnp.float32
BF = jnp.bfloat16
MESH = pl.DeviceIdType.MESH
CH = 256
ANY = pl.BlockSpec(memory_space=pl.ANY)


def dot(a, b):
    return jnp.dot(a, b, preferred_element_type=F32)


def dot_nt(a, b):
    return lax.dot_general(a, b, (((1,), (1,)), ((), ())), preferred_element_type=F32)


def dot_tn(a, b):
    return lax.dot_general(a, b, (((0,), (0,)), ((), ())), preferred_element_type=F32)


def remote(src, dst, send, recv, device):
    return pltpu.make_async_remote_copy(
        src_ref=src, dst_ref=dst, send_sem=send, recv_sem=recv,
        device_id=device, device_id_type=MESH,
    )


def greet(devices):
    barrier = pltpu.get_barrier_semaphore()
    for device in devices:
        pl.semaphore_signal(barrier, inc=1, device_id=device, device_id_type=MESH)
    pl.semaphore_wait(barrier, len(devices))


FAR = (4, 3, 5, 2, 6, 1, 7)
NEAR = (1, 7, 2, 6, 3, 5, 4)
ROWS = 1024


def total_of(*parts):
    out = parts[0].astype(F32)
    for part in parts[1:]:
        out = out + part.astype(F32)
    return out


def layer_kernel(
    length_ref, xp_h, xr_h, w_h, qp_h, qr_h, dop_h, dor_h,
    op_h, or_h, gqp_h, gqr_h, gxp_h, gxr_h, gw_h,
    xp, xr, wv, qp, qr, dop, dor, op, out_r, gqp, gqr, gxp, gxr, gw,
    kvp, kvr, kt, xrt, xs, xg, wr,
    ws, e_ref, qs, dos, qts, dots, dl, acc,
    blk, t1r, own, dkg, gp, gr, dkr,
    pbuf, prcv, x_s, x_r, z_f, z_s, z_r, pf, pb, pr,
    loc, kv_ss, kv_rs, f_ss, f_rs, w_ss, w_rs, xg_ss, xg_rs, t_ss, t_rs, a_ss, a_rs,
    y_ss, y_rs, o_ss, o_rs, p_ss, p_rs, x_ss, x_rs, z_ss, z_rs, g_ss, g_rs,
):
    d, h = lax.axis_index("dp"), lax.axis_index("head")
    p = lax.axis_index("pool")
    z, c = p // 2, p % 2
    s = 1 - 2 * c
    at_p = lambda k: (d, lax.rem(p + k, 16), h)
    at_z = lambda k: (d, lax.rem(z + k, 8) * 2 + c, h)
    at_x = lambda k: (lax.rem(d + 4 + k, 4), p, h)
    at_y = lambda k: (d, p, lax.rem(h + k, 4))
    sibling = (d, z * 2 + 1 - c, h)
    started, local = [], []

    def send(*args):
        copy = remote(*args)
        copy.start()
        started.append(copy)
        return copy

    def move(i, a, b):
        copy = pltpu.make_async_copy(a, b, loc.at[i])
        copy.start()
        return copy

    def take(region, sem):
        remote(region, region, z_ss.at[0], sem, sibling).wait_recv()

    loads = [move(i, a, b) for i, (a, b) in enumerate(
        ((xp_h, xp), (w_h, wv), (xr_h, xr), (qr_h, qr), (dor_h, dor), (qp_h, qp), (dop_h, dop)))]
    barrier = pltpu.get_barrier_semaphore()
    peers = [at_p(k) for k in range(1, 16)] + [at_x(k) for k in (1, 2, 3)] + [at_y(k) for k in (1, 2, 3)]
    for peer in peers:
        pl.semaphore_signal(barrier, inc=1, device_id=peer, device_id_type=MESH)

    lane = lax.broadcasted_iota(jnp.int32, (1, 2 * HD), 1)
    fold = jnp.where(lane < HD, KFOLD, 1.0).astype(F32)
    loads[0].wait()
    loads[1].wait()
    mine = (dot(xp[...], wv[...]) * fold).astype(BF)
    for j in range(4):
        kvp[j, p] = mine[16 * j:16 * j + 16]
    pl.semaphore_wait(barrier, len(peers))
    for k in FAR:
        send(kvp.at[:, p], kvp.at[:, p], kv_ss.at[k], kv_rs.at[k], at_z(k))
    send(kvp.at[:, p], kvp.at[:, p], kv_ss.at[0], kv_rs.at[0], sibling)
    for k in (2, 1, 3):
        rows = pl.ds(pl.multiple_of(lax.rem(h + k, 4) * 1024, 1024), 1024)
        send(wv.at[rows], wr.at[k], w_ss.at[k], w_rs.at[k], at_y(k))
    loads[2].wait()
    kvr[...] = (dot(xr[...], wv[...]) * fold).astype(BF)
    kt[:, 1024:] = kvr[...].T
    for b in range(16):
        lanes = [(q * 8 + b // 2) * 128 + (b % 2) * 64 for q in range(4)]
        xs[b] = jnp.concatenate([xp[:, i:i + 64] for i in lanes], axis=1)
    xg[0] = xs[p]
    for i in range(16):
        xrt[i * 256:(i + 1) * 256, :] = xr[:, i * 256:(i + 1) * 256].T
    for k in NEAR:
        came = lax.rem(z + 8 - k, 8) * 2 + c
        take(kvp.at[:, came], kv_rs.at[k])
        send(kvp.at[:, came], kvp.at[:, came], f_ss.at[k], f_rs.at[k], sibling)
    take(kvp.at[:, z * 2 + 1 - c], kv_rs.at[0])
    for k in NEAR:
        take(kvp.at[:, lax.rem(z + 8 - k, 8) * 2 + 1 - c], f_rs.at[k])
    for k in (8, 7, 9, 6, 10, 5, 11, 4, 12, 3, 13, 2, 14, 1, 15):
        send(xs.at[lax.rem(p + k, 16)], xg.at[k], xg_ss.at[k], xg_rs.at[0], at_p(k))
    for j in range(4):
        kt[:, j * CH:(j + 1) * CH] = kvp[j].reshape(CH, 2 * HD).T

    def kv_of(j):
        return kvr[...] if j == 4 else kvp[j].reshape(CH, 2 * HD)

    length, offset = length_ref[0, 0], p * 64

    def forward(start, q, do, chunks, mask_of):
        rows = pl.ds(start, ROWS)
        qs[rows, :] = q
        dos[rows, :] = do
        qts[:, rows] = q.T
        dots[:, rows] = do.T
        total = jnp.zeros((ROWS, 128), F32)
        for j in range(chunks):
            e = jnp.exp2(dot(q, kt[0:HD, j * CH:(j + 1) * CH]))
            mask = mask_of(j)
            if mask is not None:
                e = jnp.where(mask, e, 0.0)
            e_ref[:, j * CH:(j + 1) * CH] = e
            total = total + e[:, :128] + e[:, 128:]
        inverse = 1.0 / jnp.sum(total, axis=1, keepdims=True)
        out = jnp.zeros((ROWS, HD), F32)
        for j in range(chunks):
            weights = (e_ref[:, j * CH:(j + 1) * CH] * inverse).astype(BF)
            ws[rows, j * CH:(j + 1) * CH] = weights
            out = out + dot(weights, kv_of(j)[:, HD:])
        out = out.astype(BF)
        delta = jnp.sum(do.astype(F32) * out.astype(F32), axis=1, keepdims=True)
        dl[rows, :] = jnp.broadcast_to(delta, (ROWS, 128))
        return out

    def resp_mask(j):
        if j < 4:
            return None
        row = lax.broadcasted_iota(jnp.int32, (ROWS, CH), 0) & 255
        col = lax.broadcasted_iota(jnp.int32, (ROWS, CH), 1)
        return (col <= row) & (col < length)

    def prompt_mask(j):
        row = lax.broadcasted_iota(jnp.int32, (ROWS, CH), 0) & 63
        col = lax.broadcasted_iota(jnp.int32, (ROWS, CH), 1)
        return (col >> 4) * 64 + (col & 15) + 16 * j <= row + offset

    valid = lax.broadcasted_iota(jnp.int32, (256, HD), 0) < length
    for copy in loads[3:]:
        copy.wait()

    def resp_block(t, carry):
        heads = [pl.ds(pl.multiple_of((t * 4 + u) * HD, HD), HD) for u in range(4)]
        q = jnp.concatenate([qr[:, head] for head in heads], axis=0)
        do = jnp.concatenate([jnp.where(valid, dor[:, head], jnp.zeros((256, HD), BF)) for head in heads], axis=0)
        out = forward(pl.multiple_of(t * ROWS, ROWS), q, do, 5, resp_mask)
        for u in range(4):
            out_r[:, heads[u]] = out[u * 256:(u + 1) * 256]
        return carry

    lax.fori_loop(0, 4, resp_block, 0)
    local.append(move(7, out_r, or_h))
    q = jnp.concatenate([qp[:, u * HD:(u + 1) * HD] for u in range(16)], axis=0)
    do = jnp.concatenate([dop[:, u * HD:(u + 1) * HD] for u in range(16)], axis=0)
    out = forward(4 * ROWS, q, do, 4, prompt_mask)
    for u in range(16):
        op[:, u * HD:(u + 1) * HD] = out[u * 64:(u + 1) * 64]
    local.append(move(8, op, op_h))

    def backward(j, blocks):
        at = slice(j * CH, (j + 1) * CH)
        acc[...] = jnp.zeros_like(acc)

        def block(t, carry):
            rows = pl.ds(pl.multiple_of(t * ROWS, ROWS), ROWS)
            weights = ws[rows, at]
            delta = dl[rows, :]
            grad_w = dot(dos[rows, :], kt[HD:, at])
            grad_s = (weights.astype(F32) * (grad_w - jnp.concatenate([delta, delta], axis=1))).astype(BF)
            ws[rows, at] = grad_s
            acc[0:HD, :] += dot(qts[:, rows], grad_s)
            acc[HD:, :] += dot(dots[:, rows], weights)
            return carry

        lax.fori_loop(0, blocks, block, 0)
        return jnp.concatenate([acc[0:HD, :] * SCALE, acc[HD:, :]], axis=0).T.astype(BF)

    def scatter(j, part):
        blk[j] = part.reshape(16, 16, 256)
        t1r[j, 0] = blk[j, p]
        for k in (8, 7, 9, 6, 10, 5, 11, 4, 12, 3, 13, 2, 14, 1, 15):
            send(blk.at[j, lax.rem(p + k, 16)], t1r.at[j, k], t_ss.at[j, k], t_rs.at[j], at_p(k))

    def collect(j):
        take(t1r.at[j, pl.ds(1, 15)], t_rs.at[j])
        mine = total_of(*[t1r[j, k] for k in range(16)]).astype(BF)
        own[16 * j:16 * j + 16, :] = mine
        dkg[j, 0] = mine
        rows = pl.ds(16 * j, 16)
        for k in (8, 7, 9, 6, 10, 5, 11, 4, 12, 3, 13, 2, 14, 1, 15):
            send(own.at[rows], dkg.at[j, k], a_ss.at[j, k], a_rs.at[j], at_p(k))
        for k in (1, 2, 3):
            send(own.at[rows], gp.at[k, rows], o_ss.at[j, k], o_rs.at[k], at_y(k))

    dkr[...] = backward(4, 4)
    for k in (1, 2, 3):
        send(dkr, gr.at[k], y_ss.at[k], y_rs.at[k], at_y(k))
    order = (2, 1, 3, 0)
    for i, r in enumerate(order):
        rows = pl.ds(pl.multiple_of(lax.rem(d + r, 4) * 1024, 1024), 1024)
        piece = dot(xrt[rows, :], dkr[...]).astype(BF)
        for b in range(16):
            pbuf[i, b % 2, b // 2] = piece[b * 64:(b + 1) * 64]
        send(pbuf.at[i, 1 - c], prcv.at[i], p_ss.at[i], p_rs.at[i], sibling)
    direct, summed = 2 - c, 1 + c

    scatter(0, backward(0, 5))
    take(prcv.at[0], p_rs.at[0])
    x_s[0] = total_of(pbuf[0, c], prcv[0]).astype(BF)
    send(x_s.at[0], x_r.at[0], x_ss.at[0], x_rs.at[0], at_x(s))
    take(prcv.at[direct], p_rs.at[direct])
    x_s[1] = total_of(pbuf[direct, c], prcv[direct]).astype(BF)
    send(x_s.at[1], x_r.at[1], x_ss.at[1], x_rs.at[1], at_x(-s))

    scatter(1, backward(1, 5))
    collect(0)
    take(prcv.at[summed], p_rs.at[summed])
    take(x_r.at[0], x_rs.at[0])
    x_s[2] = total_of(pbuf[summed, c], prcv[summed], x_r[0]).astype(BF)
    send(x_s.at[2], x_r.at[2], x_ss.at[2], x_rs.at[2], at_x(s))

    scatter(2, backward(2, 5))
    collect(1)
    take(prcv.at[3], p_rs.at[3])
    take(x_r.at[1], x_rs.at[1])
    take(x_r.at[2], x_rs.at[2])
    z_f[...] = total_of(pbuf[3, c], prcv[3], x_r[1], x_r[2])
    z_s[...] = z_f[...].astype(BF)
    for k in FAR:
        send(z_s.at[lax.rem(z + k, 8)], z_r.at[k], z_ss.at[k], z_rs.at[k], at_z(k))

    scatter(3, backward(3, 5))
    collect(2)

    def grad_q_block(t, carry):
        rows = pl.ds(pl.multiple_of(t * ROWS, ROWS), ROWS)
        grad_q = dot(ws[rows, 0:CH], kv_of(0)[:, 0:HD])
        for j in range(1, 5):
            grad_q = grad_q + dot(ws[rows, j * CH:(j + 1) * CH], kv_of(j)[:, 0:HD])
        grad_q = (grad_q * LN2).astype(BF)
        for u in range(4):
            gqr[:, pl.ds(pl.multiple_of((t * 4 + u) * HD, HD), HD)] = grad_q[u * 256:(u + 1) * 256]
        return carry

    lax.fori_loop(0, 2, grad_q_block, 0)
    collect(3)
    lax.fori_loop(2, 4, grad_q_block, 0)
    local.append(move(9, gqr, gqr_h))
    rows = slice(4 * ROWS, 5 * ROWS)
    grad_q = dot(ws[rows, 0:CH], kv_of(0)[:, 0:HD])
    for j in range(1, 4):
        grad_q = grad_q + dot(ws[rows, j * CH:(j + 1) * CH], kv_of(j)[:, 0:HD])
    grad_q = (grad_q * LN2).astype(BF)
    for u in range(16):
        gqp[:, u * HD:(u + 1) * HD] = grad_q[u * 64:(u + 1) * 64]
    local.append(move(10, gqp, gqp_h))

    take(xg.at[pl.ds(1, 15)], xg_rs.at[0])
    share = None
    for j in range(4):
        take(dkg.at[j, pl.ds(1, 15)], a_rs.at[j])
        part = dot_tn(xg[:, 16 * j:16 * j + 16, :].reshape(256, 256), dkg[j].reshape(256, 256))
        share = part if share is None else share + part
    pf[...] = share.reshape(4, 64, 256)
    pb[...] = share.astype(BF).reshape(4, 64, 256)
    for k in (2, 1, 3):
        send(pb.at[lax.rem(d + k, 4)], pr.at[k], g_ss.at[k], g_rs.at[k], at_x(k))

    w_own = wv[pl.ds(pl.multiple_of(h * 1024, 1024), 1024), :]
    for k in (1, 2, 3):
        take(wr.at[k], w_rs.at[k])
        take(gr.at[k], y_rs.at[k])
    gxr[...] = (dot_nt(dkr[...], w_own) + dot_nt(gr[1], wr[1]) + dot_nt(gr[2], wr[2]) + dot_nt(gr[3], wr[3])).astype(BF)
    local.append(move(11, gxr, gxr_h))
    for k in (1, 2, 3):
        take(gp.at[k], o_rs.at[k])
    gxp[...] = (dot_nt(own[...], w_own) + dot_nt(gp[1], wr[1]) + dot_nt(gp[2], wr[2]) + dot_nt(gp[3], wr[3])).astype(BF)
    local.append(move(12, gxp, gxp_h))
    for k in range(1, 8):
        take(z_r.at[k], z_rs.at[k])
    for k in (1, 2, 3):
        take(pr.at[k], g_rs.at[k])
    gw[...] = total_of(z_f[z], pf[d], *[z_r[k] for k in range(1, 8)], *[pr[k] for k in (1, 2, 3)])
    local.append(move(13, gw, gw_h))
    for copy in started:
        copy.wait_send()
    for copy in local:
        copy.wait()


def layer(length, xp, xr, w, qp, qr, dop, dor):
    dma = pltpu.SemaphoreType.DMA
    bf = lambda *shape: pltpu.VMEM(shape, BF)
    f32 = lambda *shape: pltpu.VMEM(shape, F32)
    block = (8, 64, 256)
    outs = [
        jax.ShapeDtypeStruct((64, 2048), BF), jax.ShapeDtypeStruct((256, 2048), BF),
        jax.ShapeDtypeStruct((64, 2048), BF), jax.ShapeDtypeStruct((256, 2048), BF),
        jax.ShapeDtypeStruct((64, 1024), BF), jax.ShapeDtypeStruct((256, 1024), BF),
        jax.ShapeDtypeStruct((64, 256), F32),
    ]
    return pl.pallas_call(
        layer_kernel,
        in_specs=[pl.BlockSpec(memory_space=pltpu.SMEM)] + [ANY] * 7,
        out_specs=[ANY] * 7,
        out_shape=outs,
        scratch_shapes=[
            bf(64, 4096), bf(256, 4096), bf(4096, 256), bf(64, 2048), bf(256, 2048), bf(64, 2048), bf(256, 2048),
            bf(64, 2048), bf(256, 2048), bf(64, 2048), bf(256, 2048), bf(64, 1024), bf(256, 1024), f32(64, 256),
            bf(4, 16, 16, 256), bf(256, 256), bf(256, 1280), bf(4096, 256), bf(16, 64, 256), bf(16, 64, 256),
            bf(4, 1024, 256),
            bf(5120, 1280), f32(ROWS, 1280), bf(5120, HD), bf(5120, HD), bf(HD, 5120), bf(HD, 5120),
            f32(5120, 128), f32(256, 256),
            bf(4, 16, 16, 256), bf(4, 16, 16, 256), bf(64, 256), bf(4, 16, 16, 256), bf(4, 64, 256),
            bf(4, 256, 256), bf(256, 256),
            bf(4, 2, *block), bf(4, *block), bf(3, *block), bf(3, *block), f32(*block), bf(*block), bf(*block),
            f32(4, 64, 256), bf(4, 64, 256), bf(4, 64, 256),
            dma((14,)), dma((8,)), dma((8,)), dma((8,)), dma((8,)), dma((4,)), dma((4,)), dma((16,)), dma((1,)),
            dma((4, 16)), dma((4,)), dma((4, 16)), dma((4,)),
            dma((4,)), dma((4,)), dma((4, 4)), dma((4,)), dma((4,)), dma((4,)), dma((3,)), dma((3,)),
            dma((8,)), dma((8,)), dma((4,)), dma((4,)),
        ],
        compiler_params=pltpu.CompilerParams(
            collective_id=0, has_side_effects=True, vmem_limit_bytes=60 << 20
        ),
        cost_estimate=pl.CostEstimate(
            flops=22_000_000_000, bytes_accessed=12 << 20, transcendentals=6_500_000
        ),
        name="layer",
    )(length, xp, xr, w, qp, qr, dop, dor)


def finish_kernel(*refs):
    n = len(refs) // 2
    sems = refs[-1]
    copies = [pltpu.make_async_copy(refs[i], refs[n + i], sems.at[i]) for i in range(n)]
    for copy in copies:
        copy.start()
    for copy in copies:
        copy.wait()


def finish(arrays):
    return pl.pallas_call(
        finish_kernel,
        in_specs=[ANY] * len(arrays),
        out_specs=[ANY] * len(arrays),
        out_shape=[jax.ShapeDtypeStruct(a.shape, a.dtype) for a in arrays],
        scratch_shapes=[pltpu.SemaphoreType.DMA((len(arrays),))],
        name="finish",
    )(*arrays)


def body(x_prompt, x_resp, w_kv, q_prompt, q_resp, do_prompt, do_resp, resp_len):
    arrays = layer(
        resp_len, x_prompt[0], x_resp[0], w_kv, q_prompt[0], q_resp[0], do_prompt[0], do_resp[0]
    )
    op, out_r, gqp, gqr, gxp, gxr, gw = finish(arrays)
    return op[None], out_r[None], gqp[None], gqr[None], gxp[None], gxr[None], gw


def solution(mesh):
    return jax.shard_map(
        body,
        mesh=mesh,
        in_specs=(
            P("dp", "pool", None),
            P("dp", "pool", None),
            P(None, "head"),
            P("dp", "pool", "head"),
            P("dp", "pool", "head"),
            P("dp", "pool", "head"),
            P("dp", "pool", "head"),
            P("dp", "pool"),
        ),
        out_specs=(
            P("dp", "pool", "head"),
            P("dp", "pool", "head"),
            P("dp", "pool", "head"),
            P("dp", "pool", "head"),
            P("dp", "pool", "head"),
            P("dp", "pool", "head"),
            P(("dp", "pool"), "head"),
        ),
        check_vma=False,
    )
```

```python
import math

import jax
import jax.numpy as jnp
from jax import lax
from jax.experimental import pallas as pl
from jax.experimental.pallas import tpu as pltpu
from jax.sharding import PartitionSpec as P

HD = 128
LN2 = math.log(2.0)
SCALE = 1.0 / math.sqrt(HD)
KFOLD = SCALE / LN2
F32 = jnp.float32
BF = jnp.bfloat16
MESH = pl.DeviceIdType.MESH
CH = 256
ANY = pl.BlockSpec(memory_space=pl.ANY)


def dot(a, b):
    return jnp.dot(a, b, preferred_element_type=F32)


def dot_nt(a, b):
    return lax.dot_general(a, b, (((1,), (1,)), ((), ())), preferred_element_type=F32)


def dot_tn(a, b):
    return lax.dot_general(a, b, (((0,), (0,)), ((), ())), preferred_element_type=F32)


def remote(src, dst, send, recv, device):
    return pltpu.make_async_remote_copy(
        src_ref=src, dst_ref=dst, send_sem=send, recv_sem=recv,
        device_id=device, device_id_type=MESH,
    )


FAR = (4, 3, 5, 2, 6, 1, 7)
NEAR = (1, 7, 2, 6, 3, 5, 4)
ROWS = 1024
CLUSTER = ((2, 0), (2, 1), (1, 0), (3, 0), (1, 1), (3, 1), (0, 1))


def total_of(*parts):
    out = parts[0].astype(F32)
    for part in parts[1:]:
        out = out + part.astype(F32)
    return out


def layer_kernel(
    length_ref, xp_h, xr_h, w_h, qp_h, qr_h, dop_h, dor_h,
    op_h, or_h, gqp_h, gqr_h, gxp_h, gxr_h, gw_h,
    xp, xr, wv, qp, qr, dop, dor, op, out_r, gqp, gqr, gxp, gxr, gw,
    kvp, kvr, kt, xrt, xs, xg, xgt, wr,
    ws, e_ref, e_own, qs, dos, qts, dots, dl, acc,
    blk, tpr, tsum, t1r, own, og, gp, gr, dkr,
    pbuf, prcv, x_s, x_r, z_f, z_s, z_r,
    loc, kv_ss, kv_rs, f_ss, f_rs, w_ss, w_rs, xg_ss, xg_rs, t_ss, t_rs, a_ss, a_rs,
    y_ss, y_rs, o_ss, o_rs, p_ss, p_rs, x_ss, x_rs, z_ss, z_rs, q_ss, q_rs,
):
    d, h = lax.axis_index("dp"), lax.axis_index("head")
    p = lax.axis_index("pool")
    z, c = p // 2, p % 2
    s = 1 - 2 * c
    at_dc = lambda kd, kc: (lax.rem(d + kd, 4), z * 2 + lax.rem(c + kc, 2), h)
    at_z = lambda k: (d, lax.rem(z + k, 8) * 2 + c, h)
    at_x = lambda k: (lax.rem(d + 4 + k, 4), p, h)
    at_y = lambda k: (d, p, lax.rem(h + k, 4))
    sibling = (d, z * 2 + 1 - c, h)
    started, local = [], []

    def send(*args):
        copy = remote(*args)
        copy.start()
        started.append(copy)
        return copy

    def move(i, a, b):
        copy = pltpu.make_async_copy(a, b, loc.at[i])
        copy.start()
        return copy

    def take(region, sem):
        remote(region, region, z_ss.at[0], sem, sibling).wait_recv()

    loads = [move(i, a, b) for i, (a, b) in enumerate(
        ((xp_h, xp), (w_h, wv), (xr_h, xr), (qr_h, qr), (dor_h, dor), (qp_h, qp), (dop_h, dop)))]
    barrier = pltpu.get_barrier_semaphore()
    peers = [at_z(k) for k in range(1, 8)] + [at_dc(*k) for k in CLUSTER] + [at_y(k) for k in (1, 2, 3)]
    for peer in peers:
        pl.semaphore_signal(barrier, inc=1, device_id=peer, device_id_type=MESH)

    lane = lax.broadcasted_iota(jnp.int32, (1, 2 * HD), 1)
    fold = jnp.where(lane < HD, KFOLD, 1.0).astype(F32)
    loads[0].wait()
    loads[1].wait()
    mine = (dot(xp[...], wv[...]) * fold).astype(BF)
    for j in range(4):
        kvp[j, p] = mine[16 * j:16 * j + 16]
    pl.semaphore_wait(barrier, len(peers))
    for k in FAR:
        send(kvp.at[:, p], kvp.at[:, p], kv_ss.at[k], kv_rs.at[k], at_z(k))
    send(kvp.at[:, p], kvp.at[:, p], kv_ss.at[0], kv_rs.at[0], sibling)
    for k in (2, 1, 3):
        rows = pl.ds(pl.multiple_of(lax.rem(h + k, 4) * 1024, 1024), 1024)
        send(wv.at[rows], wr.at[k], w_ss.at[k], w_rs.at[k], at_y(k))
    loads[2].wait()
    kvr[...] = (dot(xr[...], wv[...]) * fold).astype(BF)
    kt[:, 1024:] = kvr[...].T
    for q in range(4):
        for half in range(2):
            starts = [q * 1024 + b * 128 + half * 64 for b in range(8)]
            xs[q, half] = jnp.concatenate([xp[:, i:i + 64] for i in starts], axis=1)
    xg[0, 0] = xs[d, c]
    for kd, kc in CLUSTER:
        send(xs.at[lax.rem(d + kd, 4), lax.rem(c + kc, 2)], xg.at[kd, kc], xg_ss.at[kd, kc], xg_rs.at[kd, kc], at_dc(kd, kc))
    for i in range(16):
        xrt[i * 256:(i + 1) * 256, :] = xr[:, i * 256:(i + 1) * 256].T
    for copy in loads[3:]:
        copy.wait()
    length, offset = length_ref[0, 0], p * 64
    row = lax.broadcasted_iota(jnp.int32, (ROWS, CH), 0)
    col = lax.broadcasted_iota(jnp.int32, (ROWS, CH), 1)
    resp_mask = (col <= (row & 255)) & (col < length)
    valid = lax.broadcasted_iota(jnp.int32, (256, HD), 0) < length

    def keep(t, q, do):
        rows = slice(t * ROWS, (t + 1) * ROWS)
        qs[rows, :] = q
        dos[rows, :] = do
        qts[:, rows] = q.T
        dots[:, rows] = do.T

    for t in range(4):
        heads = [slice((t * 4 + u) * HD, (t * 4 + u + 1) * HD) for u in range(4)]
        q = jnp.concatenate([qr[:, head] for head in heads], axis=0)
        do = jnp.concatenate([jnp.where(valid, dor[:, head], jnp.zeros((256, HD), BF)) for head in heads], axis=0)
        keep(t, q, do)
        e_own[t * ROWS:(t + 1) * ROWS, :] = jnp.where(resp_mask, jnp.exp2(dot(q, kt[0:HD, 1024:])), 0.0)
    q = jnp.concatenate([qp[:, u * HD:(u + 1) * HD] for u in range(16)], axis=0)
    do = jnp.concatenate([dop[:, u * HD:(u + 1) * HD] for u in range(16)], axis=0)
    keep(4, q, do)
    for k in NEAR:
        came = lax.rem(z + 8 - k, 8) * 2 + c
        take(kvp.at[:, came], kv_rs.at[k])
        send(kvp.at[:, came], kvp.at[:, came], f_ss.at[k], f_rs.at[k], sibling)
    take(kvp.at[:, z * 2 + 1 - c], kv_rs.at[0])
    for k in NEAR:
        take(kvp.at[:, lax.rem(z + 8 - k, 8) * 2 + 1 - c], f_rs.at[k])
    for j in range(4):
        kt[:, j * CH:(j + 1) * CH] = kvp[j].reshape(CH, 2 * HD).T

    def kv_of(j):
        return kvr[...] if j == 4 else kvp[j].reshape(CH, 2 * HD)

    def forward(t):
        rows = slice(t * ROWS, (t + 1) * ROWS)
        q, do = qs[rows, :], dos[rows, :]
        total = jnp.zeros((ROWS, 128), F32)
        for j in range(4):
            e = jnp.exp2(dot(q, kt[0:HD, j * CH:(j + 1) * CH]))
            if t == 4:
                allowed = (col >> 4) * 64 + (col & 15) + 16 * j <= (row & 63) + offset
                e = jnp.where(allowed, e, 0.0)
            e_ref[:, j * CH:(j + 1) * CH] = e
            total = total + e[:, :128] + e[:, 128:]
        if t < 4:
            total = total + e_own[rows, :128] + e_own[rows, 128:]
        inverse = 1.0 / jnp.sum(total, axis=1, keepdims=True)
        out = jnp.zeros((ROWS, HD), F32)
        for j in range(4 if t == 4 else 5):
            e = e_own[rows, :] if j == 4 else e_ref[:, j * CH:(j + 1) * CH]
            weights = (e * inverse).astype(BF)
            ws[rows, j * CH:(j + 1) * CH] = weights
            out = out + dot(weights, kv_of(j)[:, HD:])
        out = out.astype(BF)
        delta = jnp.sum(do.astype(F32) * out.astype(F32), axis=1, keepdims=True)
        dl[rows, :] = jnp.broadcast_to(delta, (ROWS, 128))
        return out

    for t in range(4):
        out = forward(t)
        for u in range(4):
            out_r[:, (t * 4 + u) * HD:(t * 4 + u + 1) * HD] = out[u * 256:(u + 1) * 256]
    local.append(move(7, out_r, or_h))

    def backward(j, blocks):
        at = slice(j * CH, (j + 1) * CH)
        acc[...] = jnp.zeros_like(acc)

        for t in range(blocks):
            rows = slice(t * ROWS, (t + 1) * ROWS)
            weights = ws[rows, at]
            delta = dl[rows, :]
            grad_w = dot(dos[rows, :], kt[HD:, at])
            grad_s = (weights.astype(F32) * (grad_w - jnp.concatenate([delta, delta], axis=1))).astype(BF)
            ws[rows, at] = grad_s
            acc[0:HD, :] += dot(qts[:, rows], grad_s)
            acc[HD:, :] += dot(dots[:, rows], weights)
        return jnp.concatenate([acc[0:HD, :] * SCALE, acc[HD:, :]], axis=0).T.astype(BF)

    def pair_up(j, part):
        for b in range(16):
            blk[j, b % 2, b // 2] = part[b * 16:(b + 1) * 16]
        send(blk.at[j, 1 - c], tpr.at[j], q_ss.at[j], q_rs.at[j], sibling)

    def scatter(j):
        take(tpr.at[j], q_rs.at[j])
        tsum[j] = total_of(blk[j, c], tpr[j]).astype(BF)
        for k in FAR:
            send(tsum.at[j, lax.rem(z + k, 8)], t1r.at[j, k], t_ss.at[j, k], t_rs.at[j, k], at_z(k))

    def collect(j):
        for k in NEAR:
            take(t1r.at[j, k], t_rs.at[j, k])
        mine = total_of(tsum[j, z], *[t1r[j, k] for k in range(1, 8)]).astype(BF)
        rows = slice(16 * j, 16 * j + 16)
        own[rows, :] = mine
        og[0, 0, rows] = mine
        rows = pl.ds(16 * j, 16)
        for kd, kc in CLUSTER:
            send(own.at[rows], og.at[kd, kc, rows], a_ss.at[j, kd, kc], a_rs.at[j, kd, kc], at_dc(kd, kc))
        for k in (1, 2, 3):
            send(own.at[rows], gp.at[k, rows], o_ss.at[j, k], o_rs.at[k], at_y(k))

    dkr[...] = backward(4, 4)
    for k in (1, 2, 3):
        send(dkr, gr.at[k], y_ss.at[k], y_rs.at[k], at_y(k))
    order = (2, 1, 3, 0)
    for i, r in enumerate(order):
        rows = pl.ds(pl.multiple_of(lax.rem(d + r, 4) * 1024, 1024), 1024)
        piece = dot(xrt[rows, :], dkr[...]).astype(BF)
        for b in range(16):
            pbuf[i, b % 2, b // 2] = piece[b * 64:(b + 1) * 64]
        send(pbuf.at[i, 1 - c], prcv.at[i], p_ss.at[i], p_rs.at[i], sibling)
    direct, summed = 2 - c, 1 + c
    out = forward(4)
    for u in range(16):
        op[:, u * HD:(u + 1) * HD] = out[u * 64:(u + 1) * 64]
    local.append(move(8, op, op_h))
    take(prcv.at[0], p_rs.at[0])
    x_s[0] = total_of(pbuf[0, c], prcv[0]).astype(BF)
    send(x_s.at[0], x_r.at[0], x_ss.at[0], x_rs.at[0], at_x(s))

    pair_up(0, backward(0, 5))
    take(prcv.at[direct], p_rs.at[direct])
    x_s[1] = total_of(pbuf[direct, c], prcv[direct]).astype(BF)
    send(x_s.at[1], x_r.at[1], x_ss.at[1], x_rs.at[1], at_x(-s))

    pair_up(1, backward(1, 5))
    scatter(0)
    pair_up(2, backward(2, 5))
    scatter(1)
    take(prcv.at[summed], p_rs.at[summed])
    take(x_r.at[0], x_rs.at[0])
    x_s[2] = total_of(pbuf[summed, c], prcv[summed], x_r[0]).astype(BF)
    send(x_s.at[2], x_r.at[2], x_ss.at[2], x_rs.at[2], at_x(s))
    pair_up(3, backward(3, 5))
    scatter(2)
    collect(0)

    def grad_q_block(t):
        rows = slice(t * ROWS, (t + 1) * ROWS)
        grad_q = dot(ws[rows, 0:CH], kv_of(0)[:, 0:HD])
        for j in range(1, 5):
            grad_q = grad_q + dot(ws[rows, j * CH:(j + 1) * CH], kv_of(j)[:, 0:HD])
        grad_q = (grad_q * LN2).astype(BF)
        for u in range(4):
            gqr[:, (t * 4 + u) * HD:(t * 4 + u + 1) * HD] = grad_q[u * 256:(u + 1) * 256]

    grad_q_block(0)
    grad_q_block(1)
    scatter(3)
    collect(1)
    grad_q_block(2)
    collect(2)
    grad_q_block(3)
    local.append(move(9, gqr, gqr_h))
    rows = slice(4 * ROWS, 5 * ROWS)
    grad_q = dot(ws[rows, 0:CH], kv_of(0)[:, 0:HD])
    for j in range(1, 4):
        grad_q = grad_q + dot(ws[rows, j * CH:(j + 1) * CH], kv_of(j)[:, 0:HD])
    grad_q = (grad_q * LN2).astype(BF)
    for u in range(16):
        gqp[:, u * HD:(u + 1) * HD] = grad_q[u * 64:(u + 1) * 64]
    local.append(move(10, gqp, gqp_h))
    collect(3)

    for kd, kc in CLUSTER:
        take(xg.at[kd, kc], xg_rs.at[kd, kc])
    xgt[...] = xg[...].reshape(512, 512).T
    take(prcv.at[3], p_rs.at[3])
    take(x_r.at[1], x_rs.at[1])
    take(x_r.at[2], x_rs.at[2])
    z_f[...] = total_of(pbuf[3, c], prcv[3], x_r[1], x_r[2])
    for j in range(4):
        for kd, kc in CLUSTER:
            take(og.at[kd, kc, pl.ds(16 * j, 16)], a_rs.at[j, kd, kc])
    z_f[...] += dot(xgt[...], og[...].reshape(512, 256)).reshape(8, 64, 256)
    z_s[...] = z_f[...].astype(BF)
    for k in FAR:
        send(z_s.at[lax.rem(z + k, 8)], z_r.at[k], z_ss.at[k], z_rs.at[k], at_z(k))

    w_own = wv[pl.ds(pl.multiple_of(h * 1024, 1024), 1024), :]
    for k in (1, 2, 3):
        take(wr.at[k], w_rs.at[k])
        take(gr.at[k], y_rs.at[k])
    gxr[...] = (dot_nt(dkr[...], w_own) + dot_nt(gr[1], wr[1]) + dot_nt(gr[2], wr[2]) + dot_nt(gr[3], wr[3])).astype(BF)
    local.append(move(11, gxr, gxr_h))
    for k in (1, 2, 3):
        take(gp.at[k], o_rs.at[k])
    gxp[...] = (dot_nt(own[...], w_own) + dot_nt(gp[1], wr[1]) + dot_nt(gp[2], wr[2]) + dot_nt(gp[3], wr[3])).astype(BF)
    local.append(move(12, gxp, gxp_h))
    for k in range(1, 8):
        take(z_r.at[k], z_rs.at[k])
    gw[...] = total_of(z_f[z], *[z_r[k] for k in range(1, 8)])
    local.append(move(13, gw, gw_h))
    for copy in started:
        copy.wait_send()
    for copy in local:
        copy.wait()


def layer(length, xp, xr, w, qp, qr, dop, dor):
    dma = pltpu.SemaphoreType.DMA
    bf = lambda *shape: pltpu.VMEM(shape, BF)
    f32 = lambda *shape: pltpu.VMEM(shape, F32)
    block = (8, 64, 256)
    outs = [
        jax.ShapeDtypeStruct((64, 2048), BF), jax.ShapeDtypeStruct((256, 2048), BF),
        jax.ShapeDtypeStruct((64, 2048), BF), jax.ShapeDtypeStruct((256, 2048), BF),
        jax.ShapeDtypeStruct((64, 1024), BF), jax.ShapeDtypeStruct((256, 1024), BF),
        jax.ShapeDtypeStruct((64, 256), F32),
    ]
    return pl.pallas_call(
        layer_kernel,
        in_specs=[pl.BlockSpec(memory_space=pltpu.SMEM)] + [ANY] * 7,
        out_specs=[ANY] * 7,
        out_shape=outs,
        scratch_shapes=[
            bf(64, 4096), bf(256, 4096), bf(4096, 256), bf(64, 2048), bf(256, 2048), bf(64, 2048), bf(256, 2048),
            bf(64, 2048), bf(256, 2048), bf(64, 2048), bf(256, 2048), bf(64, 1024), bf(256, 1024), f32(64, 256),
            bf(4, 16, 16, 256), bf(256, 256), bf(256, 1280), bf(4096, 256), bf(4, 2, 64, 512), bf(4, 2, 64, 512),
            bf(512, 512),            bf(4, 1024, 256),
            bf(5120, 1280), f32(ROWS, 1024), f32(4 * ROWS, CH), bf(5120, HD), bf(5120, HD), bf(HD, 5120), bf(HD, 5120),
            f32(5120, 128), f32(256, 256),
            bf(4, 2, 8, 16, 256), bf(4, 8, 16, 256), bf(4, 8, 16, 256), bf(4, 8, 16, 256), bf(64, 256),
            bf(4, 2, 64, 256), bf(4, 64, 256),
            bf(4, 256, 256), bf(256, 256),
            bf(4, 2, *block), bf(4, *block), bf(3, *block), bf(3, *block), f32(*block), bf(*block), bf(*block),
            dma((14,)), dma((8,)), dma((8,)), dma((8,)), dma((8,)), dma((4,)), dma((4,)), dma((4, 2)), dma((4, 2)),
            dma((4, 8)), dma((4, 8)), dma((4, 4, 2)), dma((4, 4, 2)),
            dma((4,)), dma((4,)), dma((4, 4)), dma((4,)), dma((4,)), dma((4,)), dma((3,)), dma((3,)),
            dma((8,)), dma((8,)), dma((4,)), dma((4,)),
        ],
        compiler_params=pltpu.CompilerParams(
            collective_id=0, has_side_effects=True, vmem_limit_bytes=60 << 20
        ),
        cost_estimate=pl.CostEstimate(
            flops=22_000_000_000, bytes_accessed=12 << 20, transcendentals=6_500_000
        ),
        name="layer",
    )(length, xp, xr, w, qp, qr, dop, dor)


def finish_kernel(*refs):
    n = len(refs[:-2]) // 3
    came, went = refs[-2:]
    ins, outs, held = refs[:n], refs[n:2 * n], refs[2 * n:3 * n]
    reads = [pltpu.make_async_copy(ins[i], held[i], came.at[i]) for i in range(n)]
    writes = [pltpu.make_async_copy(held[i], outs[i], went.at[i]) for i in range(n)]
    for copy in reads:
        copy.start()
    for i in range(n):
        reads[i].wait()
        writes[i].start()
    for copy in writes:
        copy.wait()


def finish(arrays):
    n = len(arrays)
    return pl.pallas_call(
        finish_kernel,
        in_specs=[ANY] * n,
        out_specs=[ANY] * n,
        out_shape=[jax.ShapeDtypeStruct(a.shape, a.dtype) for a in arrays],
        scratch_shapes=[pltpu.VMEM(a.shape, a.dtype) for a in arrays] + [pltpu.SemaphoreType.DMA((n,))] * 2,
        name="finish",
    )(*arrays)


def body(x_prompt, x_resp, w_kv, q_prompt, q_resp, do_prompt, do_resp, resp_len):
    arrays = layer(
        resp_len, x_prompt[0], x_resp[0], w_kv, q_prompt[0], q_resp[0], do_prompt[0], do_resp[0]
    )
    op, out_r, gqp, gqr, gxp, gxr, gw = finish(arrays)
    return op[None], out_r[None], gqp[None], gqr[None], gxp[None], gxr[None], gw


def solution(mesh):
    return jax.shard_map(
        body,
        mesh=mesh,
        in_specs=(
            P("dp", "pool", None),
            P("dp", "pool", None),
            P(None, "head"),
            P("dp", "pool", "head"),
            P("dp", "pool", "head"),
            P("dp", "pool", "head"),
            P("dp", "pool", "head"),
            P("dp", "pool"),
        ),
        out_specs=(
            P("dp", "pool", "head"),
            P("dp", "pool", "head"),
            P("dp", "pool", "head"),
            P("dp", "pool", "head"),
            P("dp", "pool", "head"),
            P("dp", "pool", "head"),
            P(("dp", "pool"), "head"),
        ),
        check_vma=False,
    )
```

```python
import math

import jax
import jax.numpy as jnp
from jax import lax
from jax.experimental import pallas as pl
from jax.experimental.pallas import tpu as pltpu
from jax.sharding import PartitionSpec as P

HD = 128
LN2 = math.log(2.0)
SCALE = 1.0 / math.sqrt(HD)
KFOLD = SCALE / LN2
F32 = jnp.float32
BF = jnp.bfloat16
MESH = pl.DeviceIdType.MESH
CH = 256
ANY = pl.BlockSpec(memory_space=pl.ANY)


def dot(a, b):
    return jnp.dot(a, b, preferred_element_type=F32)


def dot_nt(a, b):
    return lax.dot_general(a, b, (((1,), (1,)), ((), ())), preferred_element_type=F32)


def dot_tn(a, b):
    return lax.dot_general(a, b, (((0,), (0,)), ((), ())), preferred_element_type=F32)


def remote(src, dst, send, recv, device):
    return pltpu.make_async_remote_copy(
        src_ref=src, dst_ref=dst, send_sem=send, recv_sem=recv,
        device_id=device, device_id_type=MESH,
    )


FAR = (4, 3, 5, 2, 6, 1, 7)
NEAR = (1, 7, 2, 6, 3, 5, 4)
ROWS = 1024
CLUSTER = ((2, 0), (2, 1), (1, 0), (3, 0), (1, 1), (3, 1), (0, 1))


def total_of(*parts):
    out = parts[0].astype(F32)
    for part in parts[1:]:
        out = out + part.astype(F32)
    return out


def layer_kernel(
    length_h, xp_h, xr_h, w_h, qp_h, qr_h, dop_h, dor_h,
    op_h, or_h, gqp_h, gqr_h, gxp_h, gxr_h, gw_h,
    length_ref, xp, xr, wv, qp, qr, dop, dor, op, out_r, gqp, gqr, gxp, gxr, gw,
    kvp, kvr, kt, xrt, xs, xg, xgt, wr,
    ws, e_ref, e_own, qs, dos, qts, dots, dl, acc,
    blk, tpr, tsum, t1r, own, og, gp, gr, dkr,
    pbuf, prcv, x_s, x_r, z_f, z_s, z_r, z_m,
    loc, kv_ss, kv_rs, f_ss, f_rs, w_ss, w_rs, xg_ss, xg_rs, t_ss, t_rs, a_ss, a_rs,
    y_ss, y_rs, o_ss, o_rs, p_ss, p_rs, x_ss, x_rs, z_ss, z_rs, q_ss, q_rs,
):
    d, h = lax.axis_index("dp"), lax.axis_index("head")
    p = lax.axis_index("pool")
    z, c = p // 2, p % 2
    s = 1 - 2 * c
    at_dc = lambda kd, kc: (lax.rem(d + kd, 4), z * 2 + lax.rem(c + kc, 2), h)
    at_z = lambda k: (d, lax.rem(z + 8 + k, 8) * 2 + c, h)
    at_x = lambda k: (lax.rem(d + 4 + k, 4), p, h)
    at_y = lambda k: (d, p, lax.rem(h + k, 4))
    sibling = (d, z * 2 + 1 - c, h)
    started, local = [], []

    def send(*args):
        copy = remote(*args)
        copy.start()
        started.append(copy)
        return copy

    def move(i, a, b):
        copy = pltpu.make_async_copy(a, b, loc.at[i])
        copy.start()
        return copy

    def take(region, sem):
        remote(region, region, z_ss.at[0], sem, sibling).wait_recv()

    loads = [move(i, a, b) for i, (a, b) in enumerate(
        ((xp_h, xp), (w_h, wv), (xr_h, xr), (qr_h, qr), (dor_h, dor), (qp_h, qp), (dop_h, dop), (length_h, length_ref)))]
    barrier = pltpu.get_barrier_semaphore()
    peers = [at_z(k) for k in range(1, 8)] + [at_dc(*k) for k in CLUSTER] + [at_y(k) for k in (1, 2, 3)]
    for peer in peers:
        pl.semaphore_signal(barrier, inc=1, device_id=peer, device_id_type=MESH)

    lane = lax.broadcasted_iota(jnp.int32, (1, 2 * HD), 1)
    fold = jnp.where(lane < HD, KFOLD, 1.0).astype(F32)
    loads[0].wait()
    loads[1].wait()
    mine = (dot(xp[...], wv[...]) * fold).astype(BF)
    for j in range(4):
        kvp[j, p] = mine[16 * j:16 * j + 16]
    pl.semaphore_wait(barrier, len(peers))
    for k in (2, 6, 1, 7):
        send(kvp.at[:, p], kvp.at[:, p], kv_ss.at[k], kv_rs.at[k], at_z(k))
    send(kvp.at[:, p], kvp.at[:, p], kv_ss.at[0], kv_rs.at[0], sibling)
    for k in (2, 1, 3):
        rows = pl.ds(pl.multiple_of(lax.rem(h + k, 4) * 1024, 1024), 1024)
        send(wv.at[rows], wr.at[k], w_ss.at[k], w_rs.at[k], at_y(k))
    loads[2].wait()
    kvr[...] = (dot(xr[...], wv[...]) * fold).astype(BF)
    kt[:, 1024:] = kvr[...].T
    for q in range(4):
        for half in range(2):
            starts = [q * 1024 + b * 128 + half * 64 for b in range(8)]
            xs[q, half] = jnp.concatenate([xp[:, i:i + 64] for i in starts], axis=1)
    xg[0, 0] = xs[d, c]
    for kd, kc in CLUSTER:
        send(xs.at[lax.rem(d + kd, 4), lax.rem(c + kc, 2)], xg.at[kd, kc], xg_ss.at[kd, kc], xg_rs.at[kd, kc], at_dc(kd, kc))
    for i in range(16):
        xrt[i * 256:(i + 1) * 256, :] = xr[:, i * 256:(i + 1) * 256].T
    for copy in loads[3:]:
        copy.wait()
    length, offset = length_ref[0, 0], p * 64
    row = lax.broadcasted_iota(jnp.int32, (ROWS, CH), 0)
    col = lax.broadcasted_iota(jnp.int32, (ROWS, CH), 1)
    resp_mask = (col <= (row & 255)) & (col < length)
    valid = lax.broadcasted_iota(jnp.int32, (256, HD), 0) < length

    def keep(t, q, do):
        rows = slice(t * ROWS, (t + 1) * ROWS)
        qs[rows, :] = q
        dos[rows, :] = do
        qts[:, rows] = q.T
        dots[:, rows] = do.T

    for t in range(4):
        heads = [slice((t * 4 + u) * HD, (t * 4 + u + 1) * HD) for u in range(4)]
        q = jnp.concatenate([qr[:, head] for head in heads], axis=0)
        do = jnp.concatenate([jnp.where(valid, dor[:, head], jnp.zeros((256, HD), BF)) for head in heads], axis=0)
        keep(t, q, do)
        e_own[t * ROWS:(t + 1) * ROWS, :] = jnp.where(resp_mask, jnp.exp2(dot(q, kt[0:HD, 1024:])), 0.0)
    q = jnp.concatenate([qp[:, u * HD:(u + 1) * HD] for u in range(16)], axis=0)
    do = jnp.concatenate([dop[:, u * HD:(u + 1) * HD] for u in range(16)], axis=0)
    keep(4, q, do)
    came = lambda k: kvp.at[:, lax.rem(z + 16 - k, 8) * 2 + c]
    for k, to in ((2, 1), (6, -1)):
        take(came(k), kv_rs.at[k])
        send(came(k), came(k), kv_ss.at[4 - to], kv_rs.at[4 - to], at_z(to))
    send(came(2 * s), came(2 * s), kv_ss.at[4], kv_rs.at[4], at_z(2 * s))
    for k in (2, 6, 1, 7, 3, 5, 4):
        if k not in (2, 6):
            take(came(k), kv_rs.at[k])
        send(came(k), came(k), f_ss.at[k], f_rs.at[k], sibling)
    take(kvp.at[:, z * 2 + 1 - c], kv_rs.at[0])
    for k in NEAR:
        take(kvp.at[:, lax.rem(z + 8 - k, 8) * 2 + 1 - c], f_rs.at[k])
    for j in range(4):
        kt[:, j * CH:(j + 1) * CH] = kvp[j].reshape(CH, 2 * HD).T

    def kv_of(j):
        return kvr[...] if j == 4 else kvp[j].reshape(CH, 2 * HD)

    def forward(t):
        rows = slice(t * ROWS, (t + 1) * ROWS)
        q, do = qs[rows, :], dos[rows, :]
        total = jnp.zeros((ROWS, 128), F32)
        for j in range(4):
            e = jnp.exp2(dot(q, kt[0:HD, j * CH:(j + 1) * CH]))
            if t == 4:
                allowed = (col >> 4) * 64 + (col & 15) + 16 * j <= (row & 63) + offset
                e = jnp.where(allowed, e, 0.0)
            e_ref[:, j * CH:(j + 1) * CH] = e
            total = total + e[:, :128] + e[:, 128:]
        if t < 4:
            total = total + e_own[rows, :128] + e_own[rows, 128:]
        inverse = 1.0 / jnp.sum(total, axis=1, keepdims=True)
        out = jnp.zeros((ROWS, HD), F32)
        for j in range(4 if t == 4 else 5):
            e = e_own[rows, :] if j == 4 else e_ref[:, j * CH:(j + 1) * CH]
            weights = (e * inverse).astype(BF)
            ws[rows, j * CH:(j + 1) * CH] = weights
            out = out + dot(weights, kv_of(j)[:, HD:])
        out = out.astype(BF)
        delta = jnp.sum(do.astype(F32) * out.astype(F32), axis=1, keepdims=True)
        dl[rows, :] = jnp.broadcast_to(delta, (ROWS, 128))
        return out

    for t in range(4):
        out = forward(t)
        for u in range(4):
            out_r[:, (t * 4 + u) * HD:(t * 4 + u + 1) * HD] = out[u * 256:(u + 1) * 256]
    local.append(move(14, out_r, or_h))

    def backward(j, blocks):
        at = slice(j * CH, (j + 1) * CH)
        acc[...] = jnp.zeros_like(acc)

        for t in range(blocks):
            rows = slice(t * ROWS, (t + 1) * ROWS)
            weights = ws[rows, at]
            delta = dl[rows, :]
            grad_w = dot(dos[rows, :], kt[HD:, at])
            grad_s = (weights.astype(F32) * (grad_w - jnp.concatenate([delta, delta], axis=1))).astype(BF)
            ws[rows, at] = grad_s
            acc[0:HD, :] += dot(qts[:, rows], grad_s)
            acc[HD:, :] += dot(dots[:, rows], weights)
        return jnp.concatenate([acc[0:HD, :] * SCALE, acc[HD:, :]], axis=0).T.astype(BF)

    def pair_up(g, parts):
        for i, part in enumerate(parts):
            for b in range(16):
                blk[g, b % 2, b // 2, 16 * i:16 * i + 16] = part[b * 16:(b + 1) * 16]
        send(blk.at[g, 1 - c], tpr.at[g], q_ss.at[g], q_rs.at[g], sibling)

    def scatter(g):
        take(tpr.at[g], q_rs.at[g])
        tsum[g] = total_of(blk[g, c], tpr[g]).astype(BF)
        for k in FAR:
            send(tsum.at[g, lax.rem(z + k, 8)], t1r.at[g, k], t_ss.at[g, k], t_rs.at[g, k], at_z(k))

    def collect(g):
        for k in NEAR:
            take(t1r.at[g, k], t_rs.at[g, k])
        mine = total_of(tsum[g, z], *[t1r[g, k] for k in range(1, 8)]).astype(BF)
        own[32 * g:32 * g + 32, :] = mine
        og[0, 0, 32 * g:32 * g + 32] = mine
        rows = pl.ds(32 * g, 32)
        for kd, kc in CLUSTER:
            send(own.at[rows], og.at[kd, kc, rows], a_ss.at[g, kd, kc], a_rs.at[g, kd, kc], at_dc(kd, kc))
        for k in (1, 2, 3):
            send(own.at[rows], gp.at[k, rows], o_ss.at[g, k], o_rs.at[k], at_y(k))

    dkr[...] = backward(4, 4)
    for k in (1, 2, 3):
        send(dkr, gr.at[k], y_ss.at[k], y_rs.at[k], at_y(k))
    order = (2, 1, 3, 0)
    for i, r in enumerate(order):
        rows = pl.ds(pl.multiple_of(lax.rem(d + r, 4) * 1024, 1024), 1024)
        piece = dot(xrt[rows, :], dkr[...]).astype(BF)
        for b in range(16):
            pbuf[i, b % 2, b // 2] = piece[b * 64:(b + 1) * 64]
        send(pbuf.at[i, 1 - c], prcv.at[i], p_ss.at[i], p_rs.at[i], sibling)
    direct, summed = 2 - c, 1 + c
    out = forward(4)
    for u in range(16):
        op[:, u * HD:(u + 1) * HD] = out[u * 64:(u + 1) * 64]
    local.append(move(8, op, op_h))
    take(prcv.at[0], p_rs.at[0])
    x_s[0] = total_of(pbuf[0, c], prcv[0]).astype(BF)
    send(x_s.at[0], x_r.at[0], x_ss.at[0], x_rs.at[0], at_x(s))

    first = backward(0, 5)
    take(prcv.at[direct], p_rs.at[direct])
    x_s[1] = total_of(pbuf[direct, c], prcv[direct]).astype(BF)
    send(x_s.at[1], x_r.at[1], x_ss.at[1], x_rs.at[1], at_x(-s))
    pair_up(0, (first, backward(1, 5)))
    third = backward(2, 5)
    scatter(0)
    take(prcv.at[summed], p_rs.at[summed])
    take(x_r.at[0], x_rs.at[0])
    x_s[2] = total_of(pbuf[summed, c], prcv[summed], x_r[0]).astype(BF)
    send(x_s.at[2], x_r.at[2], x_ss.at[2], x_rs.at[2], at_x(s))
    pair_up(1, (third, backward(3, 5)))

    def grad_q_block(t):
        rows = slice(t * ROWS, (t + 1) * ROWS)
        grad_q = dot(ws[rows, 0:CH], kv_of(0)[:, 0:HD])
        for j in range(1, 5):
            grad_q = grad_q + dot(ws[rows, j * CH:(j + 1) * CH], kv_of(j)[:, 0:HD])
        grad_q = (grad_q * LN2).astype(BF)
        for u in range(4):
            gqr[:, (t * 4 + u) * HD:(t * 4 + u + 1) * HD] = grad_q[u * 256:(u + 1) * 256]

    grad_q_block(0)
    grad_q_block(1)
    scatter(1)
    collect(0)
    grad_q_block(2)
    grad_q_block(3)
    local.append(move(9, gqr, gqr_h))
    rows = slice(4 * ROWS, 5 * ROWS)
    grad_q = dot(ws[rows, 0:CH], kv_of(0)[:, 0:HD])
    for j in range(1, 4):
        grad_q = grad_q + dot(ws[rows, j * CH:(j + 1) * CH], kv_of(j)[:, 0:HD])
    grad_q = (grad_q * LN2).astype(BF)
    for u in range(16):
        gqp[:, u * HD:(u + 1) * HD] = grad_q[u * 64:(u + 1) * 64]
    local.append(move(10, gqp, gqp_h))
    collect(1)

    for kd, kc in CLUSTER:
        take(xg.at[kd, kc], xg_rs.at[kd, kc])
    xgt[...] = xg[...].reshape(512, 512).T
    take(prcv.at[3], p_rs.at[3])
    take(x_r.at[1], x_rs.at[1])
    take(x_r.at[2], x_rs.at[2])
    z_f[...] = total_of(pbuf[3, c], prcv[3], x_r[1], x_r[2])
    for g in range(2):
        for kd, kc in CLUSTER:
            take(og.at[kd, kc, pl.ds(32 * g, 32)], a_rs.at[g, kd, kc])
    z_f[...] += dot(xgt[...], og[...].reshape(512, 256)).reshape(8, 64, 256)
    z_s[...] = z_f[...].astype(BF)
    zth = lambda k: lax.rem(z + 8 + k, 8)
    for slot, block, to in ((2, 4, 2 * s), (0, 3, 1), (1, -3, -1), (3, 1, 1), (4, -1, -1)):
        send(z_s.at[zth(block)], z_r.at[slot], z_ss.at[slot], z_rs.at[slot], at_z(to))
    w_own = wv[pl.ds(pl.multiple_of(h * 1024, 1024), 1024), :]
    for k in (1, 2, 3):
        take(wr.at[k], w_rs.at[k])
        take(gr.at[k], y_rs.at[k])
    gxr[...] = (dot_nt(dkr[...], w_own) + dot_nt(gr[1], wr[1]) + dot_nt(gr[2], wr[2]) + dot_nt(gr[3], wr[3])).astype(BF)
    local.append(move(11, gxr, gxr_h))
    for slot in range(3):
        take(z_r.at[slot], z_rs.at[slot])
    z_m[0] = total_of(z_f[zth(2 * s)], z_r[c], z_r[2]).astype(BF)
    send(z_m.at[0], z_r.at[5], z_ss.at[5], z_rs.at[5], at_z(2 * s))
    z_m[1] = total_of(z_f[zth(-2 * s)], z_r[1 - c]).astype(BF)
    send(z_m.at[1], z_r.at[6], z_ss.at[6], z_rs.at[6], at_z(-2 * s))

    for k in (1, 2, 3):
        take(gp.at[k], o_rs.at[k])
    gxp[...] = (dot_nt(own[...], w_own) + dot_nt(gp[1], wr[1]) + dot_nt(gp[2], wr[2]) + dot_nt(gp[3], wr[3])).astype(BF)
    local.append(move(12, gxp, gxp_h))
    for copy in started[:-2]:
        copy.wait_send()
    for copy in local:
        copy.wait()
    for slot in (3, 4, 5, 6):
        take(z_r.at[slot], z_rs.at[slot])
    gw[...] = total_of(z_f[z], z_r[3], z_r[4], z_r[5], z_r[6])
    last = move(13, gw, gw_h)
    for copy in started[-2:]:
        copy.wait_send()
    last.wait()


def layer(length, xp, xr, w, qp, qr, dop, dor):
    dma = pltpu.SemaphoreType.DMA
    bf = lambda *shape: pltpu.VMEM(shape, BF)
    f32 = lambda *shape: pltpu.VMEM(shape, F32)
    block = (8, 64, 256)
    outs = [
        jax.ShapeDtypeStruct((64, 2048), BF), jax.ShapeDtypeStruct((256, 2048), BF),
        jax.ShapeDtypeStruct((64, 2048), BF), jax.ShapeDtypeStruct((256, 2048), BF),
        jax.ShapeDtypeStruct((64, 1024), BF), jax.ShapeDtypeStruct((256, 1024), BF),
        jax.ShapeDtypeStruct((64, 256), F32),
    ]
    return pl.pallas_call(
        layer_kernel,
        in_specs=[ANY] * 8,
        out_specs=[ANY] * 7,
        out_shape=outs,
        scratch_shapes=[
            pltpu.SMEM((1, 1), jnp.int32),
            bf(64, 4096), bf(256, 4096), bf(4096, 256), bf(64, 2048), bf(256, 2048), bf(64, 2048), bf(256, 2048),
            bf(64, 2048), bf(256, 2048), bf(64, 2048), bf(256, 2048), bf(64, 1024), bf(256, 1024), f32(64, 256),
            bf(4, 16, 16, 256), bf(256, 256), bf(256, 1280), bf(4096, 256), bf(4, 2, 64, 512), bf(4, 2, 64, 512),
            bf(512, 512),            bf(4, 1024, 256),
            bf(5120, 1280), f32(ROWS, 1024), f32(4 * ROWS, CH), bf(5120, HD), bf(5120, HD), bf(HD, 5120), bf(HD, 5120),
            f32(5120, 128), f32(256, 256),
            bf(2, 2, 8, 32, 256), bf(2, 8, 32, 256), bf(2, 8, 32, 256), bf(2, 8, 32, 256), bf(64, 256),
            bf(4, 2, 64, 256), bf(4, 64, 256),
            bf(4, 256, 256), bf(256, 256),
            bf(4, 2, *block), bf(4, *block), bf(3, *block), bf(3, *block), f32(*block), bf(*block), bf(*block), bf(2, 64, 256),
            dma((15,)), dma((8,)), dma((8,)), dma((8,)), dma((8,)), dma((4,)), dma((4,)), dma((4, 2)), dma((4, 2)),
            dma((4, 8)), dma((4, 8)), dma((4, 4, 2)), dma((4, 4, 2)),
            dma((4,)), dma((4,)), dma((4, 4)), dma((4,)), dma((4,)), dma((4,)), dma((3,)), dma((3,)),
            dma((8,)), dma((8,)), dma((4,)), dma((4,)),
        ],
        compiler_params=pltpu.CompilerParams(
            collective_id=0, has_side_effects=True, vmem_limit_bytes=60 << 20
        ),
        cost_estimate=pl.CostEstimate(
            flops=22_000_000_000, bytes_accessed=12 << 20, transcendentals=6_500_000
        ),
        name="layer",
    )(length, xp, xr, w, qp, qr, dop, dor)


def finish_kernel(*refs):
    n = len(refs[:-2]) // 3
    came, went = refs[-2:]
    ins, outs, held = refs[:n], refs[n:2 * n], refs[2 * n:3 * n]
    reads = [pltpu.make_async_copy(ins[i], held[i], came.at[i]) for i in range(n)]
    writes = [pltpu.make_async_copy(held[i], outs[i], went.at[i]) for i in range(n)]
    for copy in reads:
        copy.start()
    for i in range(n):
        reads[i].wait()
        writes[i].start()
    for copy in writes:
        copy.wait()


def finish(arrays):
    n = len(arrays)
    return pl.pallas_call(
        finish_kernel,
        in_specs=[ANY] * n,
        out_specs=[ANY] * n,
        out_shape=[jax.ShapeDtypeStruct(a.shape, a.dtype) for a in arrays],
        scratch_shapes=[pltpu.VMEM(a.shape, a.dtype) for a in arrays] + [pltpu.SemaphoreType.DMA((n,))] * 2,
        name="finish",
    )(*arrays)


def body(x_prompt, x_resp, w_kv, q_prompt, q_resp, do_prompt, do_resp, resp_len):
    arrays = layer(
        resp_len, x_prompt[0], x_resp[0], w_kv, q_prompt[0], q_resp[0], do_prompt[0], do_resp[0]
    )
    op, out_r, gqp, gqr, gxp, gxr, gw = finish(arrays)
    return op[None], out_r[None], gqp[None], gqr[None], gxp[None], gxr[None], gw


def solution(mesh):
    return jax.shard_map(
        body,
        mesh=mesh,
        in_specs=(
            P("dp", "pool", None),
            P("dp", "pool", None),
            P(None, "head"),
            P("dp", "pool", "head"),
            P("dp", "pool", "head"),
            P("dp", "pool", "head"),
            P("dp", "pool", "head"),
            P("dp", "pool"),
        ),
        out_specs=(
            P("dp", "pool", "head"),
            P("dp", "pool", "head"),
            P("dp", "pool", "head"),
            P("dp", "pool", "head"),
            P("dp", "pool", "head"),
            P("dp", "pool", "head"),
            P(("dp", "pool"), "head"),
        ),
        check_vma=False,
    )
```

```python
import math

import jax
import jax.numpy as jnp
from jax import lax
from jax.experimental import pallas as pl
from jax.experimental.pallas import tpu as pltpu
from jax.sharding import PartitionSpec as P

HD = 128
LN2 = math.log(2.0)
SCALE = 1.0 / math.sqrt(HD)
KFOLD = SCALE / LN2
F32 = jnp.float32
BF = jnp.bfloat16
MESH = pl.DeviceIdType.MESH
CH = 256
ANY = pl.BlockSpec(memory_space=pl.ANY)


def dot(a, b):
    return jnp.dot(a, b, preferred_element_type=F32)


def dot_nt(a, b):
    return lax.dot_general(a, b, (((1,), (1,)), ((), ())), preferred_element_type=F32)


def dot_tn(a, b):
    return lax.dot_general(a, b, (((0,), (0,)), ((), ())), preferred_element_type=F32)


def remote(src, dst, send, recv, device):
    return pltpu.make_async_remote_copy(
        src_ref=src, dst_ref=dst, send_sem=send, recv_sem=recv,
        device_id=device, device_id_type=MESH,
    )


ROWS = 1024
CHIPS = ((0, 1), (-1, 2), (-2, 3), (-3, 4))
CLUSTER = ((2, 0), (2, 1), (1, 0), (3, 0), (1, 1), (3, 1), (0, 1))


def total_of(*parts):
    out = parts[0].astype(F32)
    for part in parts[1:]:
        out = out + part.astype(F32)
    return out


def layer_kernel(
    length_h, xp_h, xr_h, w_h, qp_h, qr_h, dop_h, dor_h,
    op_h, or_h, gqp_h, gqr_h, gxp_h, gxr_h, gw_h,
    length_ref, xp, xr, wv, qp, qr, dop, dor, op, out_r, gqp, gqr, gxp, gxr, gw,
    kvp, kvr, kvc, kt, xrt, xs, xg, xgt, wr,
    ws, qs, dos, qts, dots, dl, acc,
    blk, tpr, tsum, t1r, own, og, gp, gr, dkr,
    pbuf, prcv, x_s, x_r, z_f, z_s, z_r, z_m,
    loc, kv_ss, kv_rs, f_ss, f_rs, w_ss, w_rs, xg_ss, xg_rs, t_ss, t_rs, a_ss, a_rs,
    y_ss, y_rs, o_ss, o_rs, p_ss, p_rs, x_ss, x_rs, z_ss, z_rs, q_ss, q_rs,
):
    d, h = lax.axis_index("dp"), lax.axis_index("head")
    p = lax.axis_index("pool")
    z, c = p // 2, p % 2
    s = 1 - 2 * c
    at_dc = lambda kd, kc: (lax.rem(d + kd, 4), z * 2 + lax.rem(c + kc, 2), h)
    at_z = lambda k: (d, lax.rem(z + 8 + k, 8) * 2 + c, h)
    at_x = lambda k: (lax.rem(d + 4 + k, 4), p, h)
    at_y = lambda k: (d, p, lax.rem(h + k, 4))
    sibling = (d, z * 2 + 1 - c, h)
    started, local = [], []

    def send(*args):
        copy = remote(*args)
        copy.start()
        started.append(copy)
        return copy

    def move(i, a, b):
        copy = pltpu.make_async_copy(a, b, loc.at[i])
        copy.start()
        return copy

    def take(region, sem):
        remote(region, region, z_ss.at[0], sem, sibling).wait_recv()

    loads = [move(i, a, b) for i, (a, b) in enumerate(
        ((xp_h, xp), (w_h, wv), (xr_h, xr), (qr_h, qr), (dor_h, dor), (qp_h, qp), (dop_h, dop), (length_h, length_ref)))]
    barrier = pltpu.get_barrier_semaphore()
    peers = [at_z(k) for k in range(1, 8)] + [at_dc(*k) for k in CLUSTER] + [at_y(k) for k in (1, 2, 3)]
    for peer in peers:
        pl.semaphore_signal(barrier, inc=1, device_id=peer, device_id_type=MESH)

    lane = lax.broadcasted_iota(jnp.int32, (1, 2 * HD), 1)
    fold = jnp.where(lane < HD, KFOLD, 1.0).astype(F32)
    loads[0].wait()
    loads[1].wait()
    mine = (dot(xp[...], wv[...]) * fold).astype(BF)
    kvp[z, c] = mine
    pl.semaphore_wait(barrier, len(peers))
    for k in (2, 6, 1, 7):
        send(kvp.at[z, c], kvp.at[z, c], kv_ss.at[k], kv_rs.at[k], at_z(k))
    send(kvp.at[z, c], kvp.at[z, c], kv_ss.at[0], kv_rs.at[0], sibling)
    for k in (2, 1, 3):
        rows = pl.ds(pl.multiple_of(lax.rem(h + k, 4) * 1024, 1024), 1024)
        send(wv.at[rows], wr.at[k], w_ss.at[k], w_rs.at[k], at_y(k))
    loads[2].wait()
    kvr[...] = (dot(xr[...], wv[...]) * fold).astype(BF)
    kt[:, 1024:] = kvr[...].T
    for q in range(4):
        for half in range(2):
            starts = [q * 1024 + b * 128 + half * 64 for b in range(8)]
            xs[q, half] = jnp.concatenate([xp[:, i:i + 64] for i in starts], axis=1)
    xg[0, 0] = xs[d, c]
    for kd, kc in CLUSTER:
        send(xs.at[lax.rem(d + kd, 4), lax.rem(c + kc, 2)], xg.at[kd, kc], xg_ss.at[kd, kc], xg_rs.at[kd, kc], at_dc(kd, kc))
    for i in range(16):
        xrt[i * 256:(i + 1) * 256, :] = xr[:, i * 256:(i + 1) * 256].T
    for copy in loads[3:]:
        copy.wait()
    length, offset = length_ref[0, 0], p * 64
    row = lax.broadcasted_iota(jnp.int32, (ROWS, CH), 0)
    col = lax.broadcasted_iota(jnp.int32, (ROWS, CH), 1)
    resp_mask = (col <= (row & 255)) & (col < length)
    valid = lax.broadcasted_iota(jnp.int32, (256, HD), 0) < length

    def keep(t, q, do):
        rows = slice(t * ROWS, (t + 1) * ROWS)
        qs[rows, :] = q
        dos[rows, :] = do
        qts[:, rows] = q.T
        dots[:, rows] = do.T

    dl[4 * ROWS:, :] = jnp.zeros((ROWS, 128), F32)
    for t in range(4):
        heads = [slice((t * 4 + u) * HD, (t * 4 + u + 1) * HD) for u in range(4)]
        q = jnp.concatenate([qr[:, head] for head in heads], axis=0)
        do = jnp.concatenate([jnp.where(valid, dor[:, head], jnp.zeros((256, HD), BF)) for head in heads], axis=0)
        keep(t, q, do)
        rows = slice(t * ROWS, (t + 1) * ROWS)
        e = jnp.where(resp_mask, jnp.exp2(dot(q, kt[0:HD, 1024:])), 0.0)
        ws[rows, 1024:] = e.astype(BF)
        dl[rows, :] = e[:, :128] + e[:, 128:]
    q = jnp.concatenate([qp[:, u * HD:(u + 1) * HD] for u in range(16)], axis=0)
    do = jnp.concatenate([dop[:, u * HD:(u + 1) * HD] for u in range(16)], axis=0)
    keep(4, q, do)
    came = lambda k: kvp.at[lax.rem(z + 16 - k, 8), c]
    zth = lambda k: lax.rem(z + 8 + k, 8)

    def across(k):
        send(came(k), came(k), f_ss.at[k], f_rs.at[k], sibling)

    def crossed(k):
        take(kvp.at[zth(-k), 1 - c], f_rs.at[k])

    def scores(j):
        near, far = (zth(k) for k in CHIPS[j])
        at = slice(j * CH, (j + 1) * CH)
        kvc[j] = jnp.concatenate([kvp[near].reshape(128, 256), kvp[far].reshape(128, 256)], axis=0)
        kt[:, at] = kvc[j].T
        for t in range(5):
            rows = slice(t * ROWS, (t + 1) * ROWS)
            e = jnp.exp2(dot(qs[rows, :], kt[0:HD, at]))
            if t == 4:
                place = jnp.where(col < 128, near * 128, far * 128) + (col & 127)
                e = jnp.where(place <= (row & 63) + offset, e, 0.0)
            ws[rows, at] = e.astype(BF)
            dl[rows, :] += e[:, :128] + e[:, 128:]

    for k, to in ((2, 1), (6, -1)):
        take(came(k), kv_rs.at[k])
        send(came(k), came(k), kv_ss.at[4 - to], kv_rs.at[4 - to], at_z(to))
    send(came(2 * s), came(2 * s), kv_ss.at[4], kv_rs.at[4], at_z(2 * s))
    for k in (7, 1):
        take(came(k), kv_rs.at[k])
        across(k)
    across(6)
    across(2)
    take(kvp.at[z, 1 - c], kv_rs.at[0])
    crossed(7)
    scores(0)
    crossed(1)
    crossed(6)
    scores(1)
    for k in (5, 3, 4):
        take(came(k), kv_rs.at[k])
        across(k)
    crossed(2)
    crossed(5)
    scores(2)
    crossed(3)
    crossed(4)
    scores(3)

    def kv_of(j):
        return kvr[...] if j == 4 else kvc[j]

    def forward(t):
        rows = slice(t * ROWS, (t + 1) * ROWS)
        do = dos[rows, :]
        inverse = 1.0 / jnp.sum(dl[rows, :], axis=1, keepdims=True)
        out = jnp.zeros((ROWS, HD), F32)
        for j in range(4 if t == 4 else 5):
            at = slice(j * CH, (j + 1) * CH)
            weights = (ws[rows, at].astype(F32) * inverse).astype(BF)
            ws[rows, at] = weights
            out = out + dot(weights, kv_of(j)[:, HD:])
        out = out.astype(BF)
        delta = jnp.sum(do.astype(F32) * out.astype(F32), axis=1, keepdims=True)
        dl[rows, :] = jnp.broadcast_to(delta, (ROWS, 128))
        return out

    for t in range(4):
        out = forward(t)
        for u in range(4):
            out_r[:, (t * 4 + u) * HD:(t * 4 + u + 1) * HD] = out[u * 256:(u + 1) * 256]
    local.append(move(14, out_r, or_h))

    def backward(j, blocks):
        at = slice(j * CH, (j + 1) * CH)
        acc[...] = jnp.zeros_like(acc)

        for t in range(blocks):
            rows = slice(t * ROWS, (t + 1) * ROWS)
            weights = ws[rows, at]
            delta = dl[rows, :]
            grad_w = dot(dos[rows, :], kt[HD:, at])
            grad_s = (weights.astype(F32) * (grad_w - jnp.concatenate([delta, delta], axis=1))).astype(BF)
            ws[rows, at] = grad_s
            acc[0:HD, :] += dot(qts[:, rows], grad_s)
            acc[HD:, :] += dot(dots[:, rows], weights)
        return jnp.concatenate([acc[0:HD, :] * SCALE, acc[HD:, :]], axis=0).T.astype(BF)

    def pair_up(j, part):
        for i in range(4):
            blk[j, i % 2, i // 2] = part[64 * i:64 * i + 64]
        send(blk.at[j, 1 - c], tpr.at[j], q_ss.at[j], q_rs.at[j], sibling)

    def scatter(j):
        take(tpr.at[j], q_rs.at[j])
        tsum[j] = total_of(blk[j, c], tpr[j]).astype(BF)
        for i, k in enumerate(CHIPS[j]):
            if k != 0:
                send(tsum.at[j, i], t1r.at[k % 8], t_ss.at[k % 8], t_rs.at[k % 8], at_z(k))

    def collect():
        for k in range(1, 8):
            take(t1r.at[k], t_rs.at[k])
        mine = total_of(tsum[0, 0], *[t1r[k] for k in range(1, 8)]).astype(BF)
        own[...] = mine
        og[0, 0] = mine
        for kd, kc in CLUSTER:
            send(own, og.at[kd, kc], a_ss.at[kd, kc], a_rs.at[kd, kc], at_dc(kd, kc))
        for k in (1, 2, 3):
            send(own, gp.at[k], o_ss.at[k], o_rs.at[k], at_y(k))

    dkr[...] = backward(4, 4)
    for k in (1, 2, 3):
        send(dkr, gr.at[k], y_ss.at[k], y_rs.at[k], at_y(k))
    order = (2, 1, 3, 0)
    for i, r in enumerate(order):
        rows = pl.ds(pl.multiple_of(lax.rem(d + r, 4) * 1024, 1024), 1024)
        piece = dot(xrt[rows, :], dkr[...]).astype(BF)
        for b in range(16):
            pbuf[i, b % 2, b // 2] = piece[b * 64:(b + 1) * 64]
        send(pbuf.at[i, 1 - c], prcv.at[i], p_ss.at[i], p_rs.at[i], sibling)
    direct, summed = 2 - c, 1 + c
    out = forward(4)
    for u in range(16):
        op[:, u * HD:(u + 1) * HD] = out[u * 64:(u + 1) * 64]
    local.append(move(8, op, op_h))
    take(prcv.at[0], p_rs.at[0])
    x_s[0] = total_of(pbuf[0, c], prcv[0]).astype(BF)
    send(x_s.at[0], x_r.at[0], x_ss.at[0], x_rs.at[0], at_x(s))

    pair_up(3, backward(3, 5))
    take(prcv.at[direct], p_rs.at[direct])
    x_s[1] = total_of(pbuf[direct, c], prcv[direct]).astype(BF)
    send(x_s.at[1], x_r.at[1], x_ss.at[1], x_rs.at[1], at_x(-s))
    pair_up(2, backward(2, 5))
    scatter(3)
    pair_up(1, backward(1, 5))
    scatter(2)
    take(prcv.at[summed], p_rs.at[summed])
    take(x_r.at[0], x_rs.at[0])
    x_s[2] = total_of(pbuf[summed, c], prcv[summed], x_r[0]).astype(BF)
    send(x_s.at[2], x_r.at[2], x_ss.at[2], x_rs.at[2], at_x(s))
    pair_up(0, backward(0, 5))
    scatter(1)

    def grad_q_block(t):
        rows = slice(t * ROWS, (t + 1) * ROWS)
        grad_q = dot(ws[rows, 0:CH], kv_of(0)[:, 0:HD])
        for j in range(1, 5):
            grad_q = grad_q + dot(ws[rows, j * CH:(j + 1) * CH], kv_of(j)[:, 0:HD])
        grad_q = (grad_q * LN2).astype(BF)
        for u in range(4):
            gqr[:, (t * 4 + u) * HD:(t * 4 + u + 1) * HD] = grad_q[u * 256:(u + 1) * 256]

    grad_q_block(0)
    grad_q_block(1)
    scatter(0)
    grad_q_block(2)
    grad_q_block(3)
    local.append(move(9, gqr, gqr_h))
    rows = slice(4 * ROWS, 5 * ROWS)
    grad_q = dot(ws[rows, 0:CH], kv_of(0)[:, 0:HD])
    for j in range(1, 4):
        grad_q = grad_q + dot(ws[rows, j * CH:(j + 1) * CH], kv_of(j)[:, 0:HD])
    grad_q = (grad_q * LN2).astype(BF)
    for u in range(16):
        gqp[:, u * HD:(u + 1) * HD] = grad_q[u * 64:(u + 1) * 64]
    local.append(move(10, gqp, gqp_h))
    collect()

    for kd, kc in CLUSTER:
        take(xg.at[kd, kc], xg_rs.at[kd, kc])
    xgt[...] = xg[...].reshape(512, 512).T
    take(prcv.at[3], p_rs.at[3])
    take(x_r.at[1], x_rs.at[1])
    take(x_r.at[2], x_rs.at[2])
    z_f[...] = total_of(pbuf[3, c], prcv[3], x_r[1], x_r[2])
    for kd, kc in CLUSTER:
        take(og.at[kd, kc], a_rs.at[kd, kc])
    z_f[...] += dot(xgt[...], og[...].reshape(512, 256)).reshape(8, 64, 256)
    z_s[...] = z_f[...].astype(BF)
    for slot, block, to in ((2, 4, 2 * s), (0, 3, 1), (1, -3, -1), (3, 1, 1), (4, -1, -1)):
        send(z_s.at[zth(block)], z_r.at[slot], z_ss.at[slot], z_rs.at[slot], at_z(to))
    w_own = wv[pl.ds(pl.multiple_of(h * 1024, 1024), 1024), :]
    for k in (1, 2, 3):
        take(wr.at[k], w_rs.at[k])
        take(gr.at[k], y_rs.at[k])
    gxr[...] = (dot_nt(dkr[...], w_own) + dot_nt(gr[1], wr[1]) + dot_nt(gr[2], wr[2]) + dot_nt(gr[3], wr[3])).astype(BF)
    local.append(move(11, gxr, gxr_h))
    for slot in range(3):
        take(z_r.at[slot], z_rs.at[slot])
    z_m[0] = total_of(z_f[zth(2 * s)], z_r[c], z_r[2]).astype(BF)
    send(z_m.at[0], z_r.at[5], z_ss.at[5], z_rs.at[5], at_z(2 * s))
    z_m[1] = total_of(z_f[zth(-2 * s)], z_r[1 - c]).astype(BF)
    send(z_m.at[1], z_r.at[6], z_ss.at[6], z_rs.at[6], at_z(-2 * s))

    for k in (1, 2, 3):
        take(gp.at[k], o_rs.at[k])
    gxp[...] = (dot_nt(own[...], w_own) + dot_nt(gp[1], wr[1]) + dot_nt(gp[2], wr[2]) + dot_nt(gp[3], wr[3])).astype(BF)
    local.append(move(12, gxp, gxp_h))
    for copy in started[:-2]:
        copy.wait_send()
    for copy in local:
        copy.wait()
    for slot in (3, 4, 5, 6):
        take(z_r.at[slot], z_rs.at[slot])
    gw[...] = total_of(z_f[z], z_r[3], z_r[4], z_r[5], z_r[6])
    last = move(13, gw, gw_h)
    for copy in started[-2:]:
        copy.wait_send()
    last.wait()


def layer(length, xp, xr, w, qp, qr, dop, dor):
    dma = pltpu.SemaphoreType.DMA
    bf = lambda *shape: pltpu.VMEM(shape, BF)
    f32 = lambda *shape: pltpu.VMEM(shape, F32)
    block = (8, 64, 256)
    outs = [
        jax.ShapeDtypeStruct((64, 2048), BF), jax.ShapeDtypeStruct((256, 2048), BF),
        jax.ShapeDtypeStruct((64, 2048), BF), jax.ShapeDtypeStruct((256, 2048), BF),
        jax.ShapeDtypeStruct((64, 1024), BF), jax.ShapeDtypeStruct((256, 1024), BF),
        jax.ShapeDtypeStruct((64, 256), F32),
    ]
    return pl.pallas_call(
        layer_kernel,
        in_specs=[ANY] * 8,
        out_specs=[ANY] * 7,
        out_shape=outs,
        scratch_shapes=[
            pltpu.SMEM((1, 1), jnp.int32),
            bf(64, 4096), bf(256, 4096), bf(4096, 256), bf(64, 2048), bf(256, 2048), bf(64, 2048), bf(256, 2048),
            bf(64, 2048), bf(256, 2048), bf(64, 2048), bf(256, 2048), bf(64, 1024), bf(256, 1024), f32(64, 256),
            bf(8, 2, 64, 256), bf(256, 256), bf(4, 256, 256), bf(256, 1280), bf(4096, 256), bf(4, 2, 64, 512), bf(4, 2, 64, 512),
            bf(512, 512),            bf(4, 1024, 256),
            bf(5120, 1280), bf(5120, HD), bf(5120, HD), bf(HD, 5120), bf(HD, 5120),
            f32(5120, 128), f32(256, 256),
            bf(4, 2, 2, 64, 256), bf(4, 2, 64, 256), bf(4, 2, 64, 256), bf(8, 64, 256), bf(64, 256),
            bf(4, 2, 64, 256), bf(4, 64, 256),
            bf(4, 256, 256), bf(256, 256),
            bf(4, 2, *block), bf(4, *block), bf(3, *block), bf(3, *block), f32(*block), bf(*block), bf(*block), bf(2, 64, 256),
            dma((15,)), dma((8,)), dma((8,)), dma((8,)), dma((8,)), dma((4,)), dma((4,)), dma((4, 2)), dma((4, 2)),
            dma((8,)), dma((8,)), dma((4, 2)), dma((4, 2)),
            dma((4,)), dma((4,)), dma((4,)), dma((4,)), dma((4,)), dma((4,)), dma((3,)), dma((3,)),
            dma((8,)), dma((8,)), dma((4,)), dma((4,)),
        ],
        compiler_params=pltpu.CompilerParams(
            collective_id=0, has_side_effects=True, vmem_limit_bytes=60 << 20
        ),
        cost_estimate=pl.CostEstimate(
            flops=22_000_000_000, bytes_accessed=12 << 20, transcendentals=6_500_000
        ),
        name="layer",
    )(length, xp, xr, w, qp, qr, dop, dor)


def finish_kernel(*refs):
    n = len(refs[:-2]) // 3
    came, went = refs[-2:]
    ins, outs, held = refs[:n], refs[n:2 * n], refs[2 * n:3 * n]
    reads = [pltpu.make_async_copy(ins[i], held[i], came.at[i]) for i in range(n)]
    writes = [pltpu.make_async_copy(held[i], outs[i], went.at[i]) for i in range(n)]
    for copy in reads:
        copy.start()
    for i in range(n):
        reads[i].wait()
        writes[i].start()
    for copy in writes:
        copy.wait()


def finish(arrays):
    n = len(arrays)
    return pl.pallas_call(
        finish_kernel,
        in_specs=[ANY] * n,
        out_specs=[ANY] * n,
        out_shape=[jax.ShapeDtypeStruct(a.shape, a.dtype) for a in arrays],
        scratch_shapes=[pltpu.VMEM(a.shape, a.dtype) for a in arrays] + [pltpu.SemaphoreType.DMA((n,))] * 2,
        name="finish",
    )(*arrays)


def body(x_prompt, x_resp, w_kv, q_prompt, q_resp, do_prompt, do_resp, resp_len):
    arrays = layer(
        resp_len, x_prompt[0], x_resp[0], w_kv, q_prompt[0], q_resp[0], do_prompt[0], do_resp[0]
    )
    op, out_r, gqp, gqr, gxp, gxr, gw = finish(arrays)
    return op[None], out_r[None], gqp[None], gqr[None], gxp[None], gxr[None], gw


def solution(mesh):
    return jax.shard_map(
        body,
        mesh=mesh,
        in_specs=(
            P("dp", "pool", None),
            P("dp", "pool", None),
            P(None, "head"),
            P("dp", "pool", "head"),
            P("dp", "pool", "head"),
            P("dp", "pool", "head"),
            P("dp", "pool", "head"),
            P("dp", "pool"),
        ),
        out_specs=(
            P("dp", "pool", "head"),
            P("dp", "pool", "head"),
            P("dp", "pool", "head"),
            P("dp", "pool", "head"),
            P("dp", "pool", "head"),
            P("dp", "pool", "head"),
            P(("dp", "pool"), "head"),
        ),
        check_vma=False,
    )
```

```python
import math

import jax
import jax.numpy as jnp
from jax import lax
from jax.experimental import pallas as pl
from jax.experimental.pallas import tpu as pltpu
from jax.sharding import PartitionSpec as P

HD = 128
LN2 = math.log(2.0)
SCALE = 1.0 / math.sqrt(HD)
KFOLD = SCALE / LN2
F32 = jnp.float32
BF = jnp.bfloat16
MESH = pl.DeviceIdType.MESH
CH = 256
ANY = pl.BlockSpec(memory_space=pl.ANY)


def dot(a, b):
    return jnp.dot(a, b, preferred_element_type=F32)


def dot_nt(a, b):
    return lax.dot_general(a, b, (((1,), (1,)), ((), ())), preferred_element_type=F32)


def dot_tn(a, b):
    return lax.dot_general(a, b, (((0,), (0,)), ((), ())), preferred_element_type=F32)


def remote(src, dst, send, recv, device):
    return pltpu.make_async_remote_copy(
        src_ref=src, dst_ref=dst, send_sem=send, recv_sem=recv,
        device_id=device, device_id_type=MESH,
    )


ROWS = 1024
CHIPS = ((0, 1), (-1, 2), (-2, 3), (-3, 4))
CLUSTER = ((2, 0), (2, 1), (1, 0), (3, 0), (1, 1), (3, 1), (0, 1))


def total_of(*parts):
    out = parts[0].astype(F32)
    for part in parts[1:]:
        out = out + part.astype(F32)
    return out


def layer_kernel(
    length_h, xp_h, xr_h, w_h, qp_h, qr_h, dop_h, dor_h,
    op_h, or_h, gqp_h, gqr_h, gxp_h, gxr_h, gw_h,
    length_ref, xp, xr, wv, qp, qr, dop, dor, op, out_r, gqp, gqr, gxp, gxr, gw,
    kvp, kvr, kvc, kt, xrt, xs, xg, xgt, wr,
    ws, qs, dos, qts, dots, dl, acc,
    blk, tpr, tsum, t1r, tnear, own, og, gp, gr, dkr,
    pbuf, prcv, x_s, x_r, z_f, z_s, z_r, z_m,
    loc, kv_ss, kv_rs, f_ss, f_rs, w_ss, w_rs, xg_ss, xg_rs, t_ss, t_rs, a_ss, a_rs,
    y_ss, y_rs, o_ss, o_rs, p_ss, p_rs, x_ss, x_rs, z_ss, z_rs, q_ss, q_rs, n_ss, n_rs,
):
    d, h = lax.axis_index("dp"), lax.axis_index("head")
    p = lax.axis_index("pool")
    z, c = p // 2, p % 2
    s = 1 - 2 * c
    at_dc = lambda kd, kc: (lax.rem(d + kd, 4), z * 2 + lax.rem(c + kc, 2), h)
    at_z = lambda k: (d, lax.rem(z + 8 + k, 8) * 2 + c, h)
    at_x = lambda k: (lax.rem(d + 4 + k, 4), p, h)
    at_y = lambda k: (d, p, lax.rem(h + k, 4))
    sibling = (d, z * 2 + 1 - c, h)
    diagonal = lambda k: (d, lax.rem(z + 8 + k, 8) * 2 + 1 - c, h)
    started, local = [], []

    def send(*args):
        copy = remote(*args)
        copy.start()
        started.append(copy)
        return copy

    def move(i, a, b):
        copy = pltpu.make_async_copy(a, b, loc.at[i])
        copy.start()
        return copy

    def take(region, sem):
        remote(region, region, z_ss.at[0], sem, sibling).wait_recv()

    loads = [move(i, a, b) for i, (a, b) in enumerate(
        ((xp_h, xp), (w_h, wv), (xr_h, xr), (qr_h, qr), (dor_h, dor), (qp_h, qp), (dop_h, dop), (length_h, length_ref)))]
    barrier = pltpu.get_barrier_semaphore()
    peers = [at_z(k) for k in range(1, 8)] + [at_dc(*k) for k in CLUSTER] + [at_y(k) for k in (1, 2, 3)]
    peers += [diagonal(1), diagonal(-1)]
    for peer in peers:
        pl.semaphore_signal(barrier, inc=1, device_id=peer, device_id_type=MESH)

    lane = lax.broadcasted_iota(jnp.int32, (1, 2 * HD), 1)
    fold = jnp.where(lane < HD, KFOLD, 1.0).astype(F32)
    loads[0].wait()
    loads[1].wait()
    mine = (dot(xp[...], wv[...]) * fold).astype(BF)
    kvp[z, c] = mine
    pl.semaphore_wait(barrier, len(peers))
    for k in (2, 6, 1, 7):
        send(kvp.at[z, c], kvp.at[z, c], kv_ss.at[k], kv_rs.at[k], at_z(k))
    send(kvp.at[z, c], kvp.at[z, c], kv_ss.at[0], kv_rs.at[0], sibling)
    for k in (2, 1, 3):
        rows = pl.ds(pl.multiple_of(lax.rem(h + k, 4) * 1024, 1024), 1024)
        send(wv.at[rows], wr.at[k], w_ss.at[k], w_rs.at[k], at_y(k))
    loads[2].wait()
    kvr[...] = (dot(xr[...], wv[...]) * fold).astype(BF)
    kt[:, 1024:] = kvr[...].T
    for copy in loads[3:]:
        copy.wait()
    length, offset = length_ref[0, 0], p * 64
    row = lax.broadcasted_iota(jnp.int32, (ROWS, CH), 0)
    col = lax.broadcasted_iota(jnp.int32, (ROWS, CH), 1)
    resp_mask = (col <= (row & 255)) & (col < length)
    valid = lax.broadcasted_iota(jnp.int32, (256, HD), 0) < length

    def keep(t, q, do):
        rows = slice(t * ROWS, (t + 1) * ROWS)
        qs[rows, :] = q
        dos[rows, :] = do
        qts[:, rows] = q.T
        dots[:, rows] = do.T

    came = lambda k: kvp.at[lax.rem(z + 16 - k, 8), c]
    zth = lambda k: lax.rem(z + 8 + k, 8)

    def across(k):
        send(came(k), came(k), f_ss.at[k], f_rs.at[k], sibling)

    def crossed(k):
        take(kvp.at[zth(-k), 1 - c], f_rs.at[k])

    def scores(j):
        near, far = (zth(k) for k in CHIPS[j])
        at = slice(j * CH, (j + 1) * CH)
        kvc[j] = jnp.concatenate([kvp[near].reshape(128, 256), kvp[far].reshape(128, 256)], axis=0)
        kt[:, at] = kvc[j].T
        for t in range(5):
            rows = slice(t * ROWS, (t + 1) * ROWS)
            e = jnp.exp2(dot(qs[rows, :], kt[0:HD, at]))
            if t == 4:
                place = jnp.where(col < 128, near * 128, far * 128) + (col & 127)
                e = jnp.where(place <= (row & 63) + offset, e, 0.0)
            ws[rows, at] = e.astype(BF)
            dl[rows, :] += e[:, :128] + e[:, 128:]

    def prepare(t):
        heads = [slice((t * 4 + u) * HD, (t * 4 + u + 1) * HD) for u in range(4)]
        q = jnp.concatenate([qr[:, head] for head in heads], axis=0)
        do = jnp.concatenate([jnp.where(valid, dor[:, head], jnp.zeros((256, HD), BF)) for head in heads], axis=0)
        keep(t, q, do)
        rows = slice(t * ROWS, (t + 1) * ROWS)
        e = jnp.where(resp_mask, jnp.exp2(dot(q, kt[0:HD, 1024:])), 0.0)
        ws[rows, 1024:] = e.astype(BF)
        dl[rows, :] = e[:, :128] + e[:, 128:]

    prepare(0)
    prepare(1)
    for k, to in ((2, 1), (6, -1)):
        take(came(k), kv_rs.at[k])
        send(came(k), came(k), kv_ss.at[4 - to], kv_rs.at[4 - to], at_z(to))
    send(came(2 * s), came(2 * s), kv_ss.at[4], kv_rs.at[4], at_z(2 * s))
    for k in (7, 1):
        take(came(k), kv_rs.at[k])
        across(k)
    across(6)
    across(2)
    prepare(2)
    prepare(3)
    dl[4 * ROWS:, :] = jnp.zeros((ROWS, 128), F32)
    q = jnp.concatenate([qp[:, u * HD:(u + 1) * HD] for u in range(16)], axis=0)
    do = jnp.concatenate([dop[:, u * HD:(u + 1) * HD] for u in range(16)], axis=0)
    keep(4, q, do)
    take(kvp.at[z, 1 - c], kv_rs.at[0])
    crossed(7)
    scores(0)
    crossed(1)
    crossed(6)
    scores(1)
    for k in (5, 3, 4):
        take(came(k), kv_rs.at[k])
        across(k)
    for q in range(4):
        for half in range(2):
            starts = [q * 1024 + b * 128 + half * 64 for b in range(8)]
            xs[q, half] = jnp.concatenate([xp[:, i:i + 64] for i in starts], axis=1)
    xg[0, 0] = xs[d, c]
    for kd, kc in CLUSTER:
        send(xs.at[lax.rem(d + kd, 4), lax.rem(c + kc, 2)], xg.at[kd, kc], xg_ss.at[kd, kc], xg_rs.at[kd, kc], at_dc(kd, kc))
    for i in range(16):
        xrt[i * 256:(i + 1) * 256, :] = xr[:, i * 256:(i + 1) * 256].T
    crossed(2)
    crossed(5)
    scores(2)
    crossed(3)
    crossed(4)
    scores(3)

    def kv_of(j):
        return kvr[...] if j == 4 else kvc[j]

    def forward(t):
        rows = slice(t * ROWS, (t + 1) * ROWS)
        do = dos[rows, :]
        inverse = 1.0 / jnp.sum(dl[rows, :], axis=1, keepdims=True)
        out = jnp.zeros((ROWS, HD), F32)
        for j in range(4 if t == 4 else 5):
            at = slice(j * CH, (j + 1) * CH)
            weights = (ws[rows, at].astype(F32) * inverse).astype(BF)
            ws[rows, at] = weights
            out = out + dot(weights, kv_of(j)[:, HD:])
        out = out.astype(BF)
        delta = jnp.sum(do.astype(F32) * out.astype(F32), axis=1, keepdims=True)
        dl[rows, :] = jnp.broadcast_to(delta, (ROWS, 128))
        return out

    for t in range(4):
        out = forward(t)
        for u in range(4):
            out_r[:, (t * 4 + u) * HD:(t * 4 + u + 1) * HD] = out[u * 256:(u + 1) * 256]
    local.append(move(14, out_r, or_h))

    def backward(j, blocks):
        at = slice(j * CH, (j + 1) * CH)
        acc[...] = jnp.zeros_like(acc)

        for t in range(blocks):
            rows = slice(t * ROWS, (t + 1) * ROWS)
            weights = ws[rows, at]
            delta = dl[rows, :]
            grad_w = dot(dos[rows, :], kt[HD:, at])
            grad_s = (weights.astype(F32) * (grad_w - jnp.concatenate([delta, delta], axis=1))).astype(BF)
            ws[rows, at] = grad_s
            acc[0:HD, :] += dot(qts[:, rows], grad_s)
            acc[HD:, :] += dot(dots[:, rows], weights)
        return jnp.concatenate([acc[0:HD, :] * SCALE, acc[HD:, :]], axis=0).T.astype(BF)

    def pair_up(j, part):
        for i in range(4):
            blk[j, i % 2, i // 2] = part[64 * i:64 * i + 64]
        send(blk.at[j, 1 - c], tpr.at[j], q_ss.at[j], q_rs.at[j], sibling)

    def scatter(j):
        take(tpr.at[j], q_rs.at[j])
        tsum[j] = total_of(blk[j, c], tpr[j]).astype(BF)
        for i, k in enumerate(CHIPS[j]):
            send(tsum.at[j, i], t1r.at[k % 8], t_ss.at[k % 8], t_rs.at[k % 8], at_z(k))

    def spread(part):
        for i in range(4):
            blk[0, i % 2, i // 2] = part[64 * i:64 * i + 64]
        send(blk.at[0, c, 1], tnear.at[0], n_ss.at[0], n_rs.at[0], at_z(1))
        send(blk.at[0, 1 - c, 1], tnear.at[1], n_ss.at[1], n_rs.at[1], diagonal(1))
        send(blk.at[0, 1 - c, 0], tnear.at[2], n_ss.at[2], n_rs.at[2], sibling)

    def collect():
        for k in range(2, 8):
            take(t1r.at[k], t_rs.at[k])
        for k in range(3):
            take(tnear.at[k], n_rs.at[k])
        mine = total_of(blk[0, c, 0], *[tnear[k] for k in range(3)], *[t1r[k] for k in range(2, 8)]).astype(BF)
        own[...] = mine
        og[0, 0] = mine
        for kd, kc in CLUSTER:
            send(own, og.at[kd, kc], a_ss.at[kd, kc], a_rs.at[kd, kc], at_dc(kd, kc))
        for k in (1, 2, 3):
            send(own, gp.at[k], o_ss.at[k], o_rs.at[k], at_y(k))

    dkr[...] = backward(4, 4)
    for k in (1, 2, 3):
        send(dkr, gr.at[k], y_ss.at[k], y_rs.at[k], at_y(k))
    order = (2, 1, 3, 0)
    for i, r in enumerate(order):
        rows = pl.ds(pl.multiple_of(lax.rem(d + r, 4) * 1024, 1024), 1024)
        piece = dot(xrt[rows, :], dkr[...]).astype(BF)
        for b in range(16):
            pbuf[i, b % 2, b // 2] = piece[b * 64:(b + 1) * 64]
        send(pbuf.at[i, 1 - c], prcv.at[i], p_ss.at[i], p_rs.at[i], sibling)
    direct, summed = 2 - c, 1 + c
    out = forward(4)
    for u in range(16):
        op[:, u * HD:(u + 1) * HD] = out[u * 64:(u + 1) * 64]
    local.append(move(8, op, op_h))
    take(prcv.at[0], p_rs.at[0])
    x_s[0] = total_of(pbuf[0, c], prcv[0]).astype(BF)
    send(x_s.at[0], x_r.at[0], x_ss.at[0], x_rs.at[0], at_x(s))

    pair_up(3, backward(3, 5))
    take(prcv.at[direct], p_rs.at[direct])
    x_s[1] = total_of(pbuf[direct, c], prcv[direct]).astype(BF)
    send(x_s.at[1], x_r.at[1], x_ss.at[1], x_rs.at[1], at_x(-s))
    pair_up(2, backward(2, 5))
    scatter(3)
    pair_up(1, backward(1, 5))
    scatter(2)
    take(prcv.at[summed], p_rs.at[summed])
    take(x_r.at[0], x_rs.at[0])
    x_s[2] = total_of(pbuf[summed, c], prcv[summed], x_r[0]).astype(BF)
    send(x_s.at[2], x_r.at[2], x_ss.at[2], x_rs.at[2], at_x(s))
    spread(backward(0, 5))
    scatter(1)

    def grad_q_block(t):
        rows = slice(t * ROWS, (t + 1) * ROWS)
        grad_q = dot(ws[rows, 0:CH], kv_of(0)[:, 0:HD])
        for j in range(1, 5):
            grad_q = grad_q + dot(ws[rows, j * CH:(j + 1) * CH], kv_of(j)[:, 0:HD])
        grad_q = (grad_q * LN2).astype(BF)
        for u in range(4):
            gqr[:, (t * 4 + u) * HD:(t * 4 + u + 1) * HD] = grad_q[u * 256:(u + 1) * 256]

    grad_q_block(0)
    grad_q_block(1)
    grad_q_block(2)
    grad_q_block(3)
    local.append(move(9, gqr, gqr_h))
    rows = slice(4 * ROWS, 5 * ROWS)
    grad_q = dot(ws[rows, 0:CH], kv_of(0)[:, 0:HD])
    for j in range(1, 4):
        grad_q = grad_q + dot(ws[rows, j * CH:(j + 1) * CH], kv_of(j)[:, 0:HD])
    grad_q = (grad_q * LN2).astype(BF)
    for u in range(16):
        gqp[:, u * HD:(u + 1) * HD] = grad_q[u * 64:(u + 1) * 64]
    local.append(move(10, gqp, gqp_h))
    collect()

    for kd, kc in CLUSTER:
        take(xg.at[kd, kc], xg_rs.at[kd, kc])
    xgt[...] = xg[...].reshape(512, 512).T
    take(prcv.at[3], p_rs.at[3])
    take(x_r.at[1], x_rs.at[1])
    take(x_r.at[2], x_rs.at[2])
    z_f[...] = total_of(pbuf[3, c], prcv[3], x_r[1], x_r[2])
    for kd, kc in CLUSTER:
        take(og.at[kd, kc], a_rs.at[kd, kc])
    z_f[...] += dot(xgt[...], og[...].reshape(512, 256)).reshape(8, 64, 256)
    z_s[...] = z_f[...].astype(BF)
    for slot, block, to in ((2, 4, 2 * s), (0, 3, 1), (1, -3, -1), (3, 1, 1), (4, -1, -1)):
        send(z_s.at[zth(block)], z_r.at[slot], z_ss.at[slot], z_rs.at[slot], at_z(to))
    w_own = wv[pl.ds(pl.multiple_of(h * 1024, 1024), 1024), :]
    for k in (1, 2, 3):
        take(wr.at[k], w_rs.at[k])
        take(gr.at[k], y_rs.at[k])
    gxr[...] = (dot_nt(dkr[...], w_own) + dot_nt(gr[1], wr[1]) + dot_nt(gr[2], wr[2]) + dot_nt(gr[3], wr[3])).astype(BF)
    local.append(move(11, gxr, gxr_h))
    for slot in range(3):
        take(z_r.at[slot], z_rs.at[slot])
    z_m[0] = total_of(z_f[zth(2 * s)], z_r[c], z_r[2]).astype(BF)
    send(z_m.at[0], z_r.at[5], z_ss.at[5], z_rs.at[5], at_z(2 * s))
    z_m[1] = total_of(z_f[zth(-2 * s)], z_r[1 - c]).astype(BF)
    send(z_m.at[1], z_r.at[6], z_ss.at[6], z_rs.at[6], at_z(-2 * s))

    for k in (1, 2, 3):
        take(gp.at[k], o_rs.at[k])
    gxp[...] = (dot_nt(own[...], w_own) + dot_nt(gp[1], wr[1]) + dot_nt(gp[2], wr[2]) + dot_nt(gp[3], wr[3])).astype(BF)
    local.append(move(12, gxp, gxp_h))
    for copy in started[:-2]:
        copy.wait_send()
    for copy in local:
        copy.wait()
    for slot in (3, 4, 5, 6):
        take(z_r.at[slot], z_rs.at[slot])
    gw[...] = total_of(z_f[z], z_r[3], z_r[4], z_r[5], z_r[6])
    last = move(13, gw, gw_h)
    for copy in started[-2:]:
        copy.wait_send()
    last.wait()


def layer(length, xp, xr, w, qp, qr, dop, dor):
    dma = pltpu.SemaphoreType.DMA
    bf = lambda *shape: pltpu.VMEM(shape, BF)
    f32 = lambda *shape: pltpu.VMEM(shape, F32)
    block = (8, 64, 256)
    outs = [
        jax.ShapeDtypeStruct((64, 2048), BF), jax.ShapeDtypeStruct((256, 2048), BF),
        jax.ShapeDtypeStruct((64, 2048), BF), jax.ShapeDtypeStruct((256, 2048), BF),
        jax.ShapeDtypeStruct((64, 1024), BF), jax.ShapeDtypeStruct((256, 1024), BF),
        jax.ShapeDtypeStruct((64, 256), F32),
    ]
    return pl.pallas_call(
        layer_kernel,
        in_specs=[ANY] * 8,
        out_specs=[ANY] * 7,
        out_shape=outs,
        scratch_shapes=[
            pltpu.SMEM((1, 1), jnp.int32),
            bf(64, 4096), bf(256, 4096), bf(4096, 256), bf(64, 2048), bf(256, 2048), bf(64, 2048), bf(256, 2048),
            bf(64, 2048), bf(256, 2048), bf(64, 2048), bf(256, 2048), bf(64, 1024), bf(256, 1024), f32(64, 256),
            bf(8, 2, 64, 256), bf(256, 256), bf(4, 256, 256), bf(256, 1280), bf(4096, 256), bf(4, 2, 64, 512), bf(4, 2, 64, 512),
            bf(512, 512),            bf(4, 1024, 256),
            bf(5120, 1280), bf(5120, HD), bf(5120, HD), bf(HD, 5120), bf(HD, 5120),
            f32(5120, 128), f32(256, 256),
            bf(4, 2, 2, 64, 256), bf(4, 2, 64, 256), bf(4, 2, 64, 256), bf(8, 64, 256), bf(3, 64, 256), bf(64, 256),
            bf(4, 2, 64, 256), bf(4, 64, 256),
            bf(4, 256, 256), bf(256, 256),
            bf(4, 2, *block), bf(4, *block), bf(3, *block), bf(3, *block), f32(*block), bf(*block), bf(*block), bf(2, 64, 256),
            dma((15,)), dma((8,)), dma((8,)), dma((8,)), dma((8,)), dma((4,)), dma((4,)), dma((4, 2)), dma((4, 2)),
            dma((8,)), dma((8,)), dma((4, 2)), dma((4, 2)),
            dma((4,)), dma((4,)), dma((4,)), dma((4,)), dma((4,)), dma((4,)), dma((3,)), dma((3,)),
            dma((8,)), dma((8,)), dma((4,)), dma((4,)), dma((3,)), dma((3,)),
        ],
        compiler_params=pltpu.CompilerParams(
            collective_id=0, has_side_effects=True, vmem_limit_bytes=60 << 20
        ),
        cost_estimate=pl.CostEstimate(
            flops=22_000_000_000, bytes_accessed=12 << 20, transcendentals=6_500_000
        ),
        name="layer",
    )(length, xp, xr, w, qp, qr, dop, dor)


def finish_kernel(*refs):
    n = len(refs[:-2]) // 3
    came, went = refs[-2:]
    ins, outs, held = refs[:n], refs[n:2 * n], refs[2 * n:3 * n]
    reads = [pltpu.make_async_copy(ins[i], held[i], came.at[i]) for i in range(n)]
    writes = [pltpu.make_async_copy(held[i], outs[i], went.at[i]) for i in range(n)]
    for copy in reads:
        copy.start()
    for i in range(n):
        reads[i].wait()
        writes[i].start()
    for copy in writes:
        copy.wait()


def finish(arrays):
    n = len(arrays)
    return pl.pallas_call(
        finish_kernel,
        in_specs=[ANY] * n,
        out_specs=[ANY] * n,
        out_shape=[jax.ShapeDtypeStruct(a.shape, a.dtype) for a in arrays],
        scratch_shapes=[pltpu.VMEM(a.shape, a.dtype) for a in arrays] + [pltpu.SemaphoreType.DMA((n,))] * 2,
        name="finish",
    )(*arrays)


def body(x_prompt, x_resp, w_kv, q_prompt, q_resp, do_prompt, do_resp, resp_len):
    arrays = layer(
        resp_len, x_prompt[0], x_resp[0], w_kv, q_prompt[0], q_resp[0], do_prompt[0], do_resp[0]
    )
    op, out_r, gqp, gqr, gxp, gxr, gw = finish(arrays)
    return op[None], out_r[None], gqp[None], gqr[None], gxp[None], gxr[None], gw


def solution(mesh):
    return jax.shard_map(
        body,
        mesh=mesh,
        in_specs=(
            P("dp", "pool", None),
            P("dp", "pool", None),
            P(None, "head"),
            P("dp", "pool", "head"),
            P("dp", "pool", "head"),
            P("dp", "pool", "head"),
            P("dp", "pool", "head"),
            P("dp", "pool"),
        ),
        out_specs=(
            P("dp", "pool", "head"),
            P("dp", "pool", "head"),
            P("dp", "pool", "head"),
            P("dp", "pool", "head"),
            P("dp", "pool", "head"),
            P("dp", "pool", "head"),
            P(("dp", "pool"), "head"),
        ),
        check_vma=False,
    )
```

```python
import math

import jax
import jax.numpy as jnp
from jax import lax
from jax.experimental import pallas as pl
from jax.experimental.pallas import tpu as pltpu
from jax.sharding import PartitionSpec as P

HD = 128
LN2 = math.log(2.0)
SCALE = 1.0 / math.sqrt(HD)
KFOLD = SCALE / LN2
F32 = jnp.float32
BF = jnp.bfloat16
MESH = pl.DeviceIdType.MESH
CH = 256
ANY = pl.BlockSpec(memory_space=pl.ANY)


def dot(a, b):
    return jnp.dot(a, b, preferred_element_type=F32)


def dot_nt(a, b):
    return lax.dot_general(a, b, (((1,), (1,)), ((), ())), preferred_element_type=F32)


def dot_tn(a, b):
    return lax.dot_general(a, b, (((0,), (0,)), ((), ())), preferred_element_type=F32)


def remote(src, dst, send, recv, device):
    return pltpu.make_async_remote_copy(
        src_ref=src, dst_ref=dst, send_sem=send, recv_sem=recv,
        device_id=device, device_id_type=MESH,
    )


ROWS = 1024
CHIPS = ((0, 1), (-1, 2), (-2, 3), (-3, 4))
CLUSTER = ((2, 0), (2, 1), (1, 0), (3, 0), (1, 1), (3, 1), (0, 1))


def total_of(*parts):
    out = parts[0].astype(F32)
    for part in parts[1:]:
        out = out + part.astype(F32)
    return out


def layer_kernel(
    length_h, xp_h, xr_h, w_h, qp_h, qr_h, dop_h, dor_h,
    op_h, or_h, gqp_h, gqr_h, gxp_h, gxr_h, gw_h,
    length_ref, xp, xr, wv, qp, qr, dop, dor, op, out_r, gqp, gqr, gxp, gxr, gw,
    kvp, kvr, kvc, kt, xrt, xs, xg, xgt, wr,
    ws, qs, dos, qts, dots, dl, acc,
    blk, tpr, tsum, t1r, tnear, own, og, gp, gr, dkr,
    pbuf, prcv, x_s, x_r, z_f, z_s, z_r, z_m,
    loc, kv_ss, kv_rs, f_ss, f_rs, w_ss, w_rs, xg_ss, xg_rs, t_ss, t_rs, a_ss, a_rs,
    y_ss, y_rs, o_ss, o_rs, p_ss, p_rs, x_ss, x_rs, z_ss, z_rs, q_ss, q_rs, n_ss, n_rs,
):
    d, h = lax.axis_index("dp"), lax.axis_index("head")
    p = lax.axis_index("pool")
    z, c = p // 2, p % 2
    s = 1 - 2 * c
    at_dc = lambda kd, kc: (lax.rem(d + kd, 4), z * 2 + lax.rem(c + kc, 2), h)
    at_z = lambda k: (d, lax.rem(z + 8 + k, 8) * 2 + c, h)
    at_x = lambda k: (lax.rem(d + 4 + k, 4), p, h)
    at_y = lambda k: (d, p, lax.rem(h + k, 4))
    sibling = (d, z * 2 + 1 - c, h)
    diagonal = lambda k: (d, lax.rem(z + 8 + k, 8) * 2 + 1 - c, h)
    started, local = [], []

    def send(*args):
        copy = remote(*args)
        copy.start()
        started.append(copy)
        return copy

    def move(i, a, b):
        copy = pltpu.make_async_copy(a, b, loc.at[i])
        copy.start()
        return copy

    def take(region, sem):
        remote(region, region, z_ss.at[0], sem, sibling).wait_recv()

    loads = [move(i, a, b) for i, (a, b) in enumerate(
        ((xp_h, xp), (w_h, wv), (xr_h, xr), (qr_h, qr), (dor_h, dor), (qp_h, qp), (dop_h, dop), (length_h, length_ref)))]
    barrier = pltpu.get_barrier_semaphore()
    peers = [at_z(k) for k in range(1, 8)] + [at_dc(*k) for k in CLUSTER] + [at_y(k) for k in (1, 2, 3)]
    peers += [diagonal(k) for k in (1, -1, 2, -2)]
    for peer in peers:
        pl.semaphore_signal(barrier, inc=1, device_id=peer, device_id_type=MESH)

    lane = lax.broadcasted_iota(jnp.int32, (1, 2 * HD), 1)
    fold = jnp.where(lane < HD, KFOLD, 1.0).astype(F32)
    loads[0].wait()
    loads[1].wait()
    mine = (dot(xp[...], wv[...]) * fold).astype(BF)
    kvp[z, c] = mine
    pl.semaphore_wait(barrier, len(peers))
    for k in (2, 6, 1, 7):
        send(kvp.at[z, c], kvp.at[z, c], kv_ss.at[k], kv_rs.at[k], at_z(k))
    send(kvp.at[z, c], kvp.at[z, c], kv_ss.at[0], kv_rs.at[0], sibling)
    for k in (2, 1, 3):
        rows = pl.ds(pl.multiple_of(lax.rem(h + k, 4) * 1024, 1024), 1024)
        send(wv.at[rows], wr.at[k], w_ss.at[k], w_rs.at[k], at_y(k))
    loads[2].wait()
    kvr[...] = (dot(xr[...], wv[...]) * fold).astype(BF)
    kt[:, 1024:] = kvr[...].T
    for copy in loads[3:]:
        copy.wait()
    length, offset = length_ref[0, 0], p * 64
    row = lax.broadcasted_iota(jnp.int32, (ROWS, CH), 0)
    col = lax.broadcasted_iota(jnp.int32, (ROWS, CH), 1)
    resp_mask = (col <= (row & 255)) & (col < length)
    valid = lax.broadcasted_iota(jnp.int32, (256, HD), 0) < length

    def keep(t, q, do):
        rows = slice(t * ROWS, (t + 1) * ROWS)
        qs[rows, :] = q
        dos[rows, :] = do
        qts[:, rows] = q.T
        dots[:, rows] = do.T

    came = lambda k: kvp.at[lax.rem(z + 16 - k, 8), c]
    zth = lambda k: lax.rem(z + 8 + k, 8)

    def across(k):
        send(came(k), came(k), f_ss.at[k], f_rs.at[k], sibling)

    def crossed(k):
        take(kvp.at[zth(-k), 1 - c], f_rs.at[k])

    def scores(j):
        near, far = (zth(k) for k in CHIPS[j])
        at = slice(j * CH, (j + 1) * CH)
        kvc[j] = jnp.concatenate([kvp[near].reshape(128, 256), kvp[far].reshape(128, 256)], axis=0)
        kt[:, at] = kvc[j].T
        for t in range(5):
            rows = slice(t * ROWS, (t + 1) * ROWS)
            e = jnp.exp2(dot(qs[rows, :], kt[0:HD, at]))
            if t == 4:
                place = jnp.where(col < 128, near * 128, far * 128) + (col & 127)
                e = jnp.where(place <= (row & 63) + offset, e, 0.0)
            ws[rows, at] = e.astype(BF)
            dl[rows, :] += e[:, :128] + e[:, 128:]

    def prepare(t):
        heads = [slice((t * 4 + u) * HD, (t * 4 + u + 1) * HD) for u in range(4)]
        q = jnp.concatenate([qr[:, head] for head in heads], axis=0)
        do = jnp.concatenate([jnp.where(valid, dor[:, head], jnp.zeros((256, HD), BF)) for head in heads], axis=0)
        keep(t, q, do)
        rows = slice(t * ROWS, (t + 1) * ROWS)
        e = jnp.where(resp_mask, jnp.exp2(dot(q, kt[0:HD, 1024:])), 0.0)
        ws[rows, 1024:] = e.astype(BF)
        dl[rows, :] = e[:, :128] + e[:, 128:]

    prepare(0)
    prepare(1)
    for k, to in ((2, 1), (6, -1)):
        take(came(k), kv_rs.at[k])
        send(came(k), came(k), kv_ss.at[4 - to], kv_rs.at[4 - to], at_z(to))
    send(came(2 * s), came(2 * s), kv_ss.at[4], kv_rs.at[4], at_z(2 * s))
    for k in (7, 1):
        take(came(k), kv_rs.at[k])
        across(k)
    across(6)
    across(2)
    prepare(2)
    prepare(3)
    dl[4 * ROWS:, :] = jnp.zeros((ROWS, 128), F32)
    q = jnp.concatenate([qp[:, u * HD:(u + 1) * HD] for u in range(16)], axis=0)
    do = jnp.concatenate([dop[:, u * HD:(u + 1) * HD] for u in range(16)], axis=0)
    keep(4, q, do)
    take(kvp.at[z, 1 - c], kv_rs.at[0])
    crossed(7)
    scores(0)
    crossed(1)
    crossed(6)
    scores(1)
    for k in (5, 3, 4):
        take(came(k), kv_rs.at[k])
        across(k)
    for q in range(4):
        for half in range(2):
            starts = [q * 1024 + b * 128 + half * 64 for b in range(8)]
            xs[q, half] = jnp.concatenate([xp[:, i:i + 64] for i in starts], axis=1)
    xg[0, 0] = xs[d, c]
    for kd, kc in CLUSTER:
        send(xs.at[lax.rem(d + kd, 4), lax.rem(c + kc, 2)], xg.at[kd, kc], xg_ss.at[kd, kc], xg_rs.at[kd, kc], at_dc(kd, kc))
    for i in range(16):
        xrt[i * 256:(i + 1) * 256, :] = xr[:, i * 256:(i + 1) * 256].T
    crossed(2)
    crossed(5)
    scores(2)
    crossed(3)
    crossed(4)
    scores(3)

    def kv_of(j):
        return kvr[...] if j == 4 else kvc[j]

    def forward(t):
        rows = slice(t * ROWS, (t + 1) * ROWS)
        do = dos[rows, :]
        inverse = 1.0 / jnp.sum(dl[rows, :], axis=1, keepdims=True)
        out = jnp.zeros((ROWS, HD), F32)
        for j in range(4 if t == 4 else 5):
            at = slice(j * CH, (j + 1) * CH)
            weights = (ws[rows, at].astype(F32) * inverse).astype(BF)
            ws[rows, at] = weights
            out = out + dot(weights, kv_of(j)[:, HD:])
        out = out.astype(BF)
        delta = jnp.sum(do.astype(F32) * out.astype(F32), axis=1, keepdims=True)
        dl[rows, :] = jnp.broadcast_to(delta, (ROWS, 128))
        return out

    for t in range(4):
        out = forward(t)
        for u in range(4):
            out_r[:, (t * 4 + u) * HD:(t * 4 + u + 1) * HD] = out[u * 256:(u + 1) * 256]
    local.append(move(14, out_r, or_h))

    def backward(j, blocks):
        at = slice(j * CH, (j + 1) * CH)
        acc[...] = jnp.zeros_like(acc)

        for t in range(blocks):
            rows = slice(t * ROWS, (t + 1) * ROWS)
            weights = ws[rows, at]
            delta = dl[rows, :]
            grad_w = dot(dos[rows, :], kt[HD:, at])
            grad_s = (weights.astype(F32) * (grad_w - jnp.concatenate([delta, delta], axis=1))).astype(BF)
            ws[rows, at] = grad_s
            acc[0:HD, :] += dot(qts[:, rows], grad_s)
            acc[HD:, :] += dot(dots[:, rows], weights)
        return jnp.concatenate([acc[0:HD, :] * SCALE, acc[HD:, :]], axis=0).T.astype(BF)

    def pair_up(j, part):
        for i in range(4):
            blk[j, i % 2, i // 2] = part[64 * i:64 * i + 64]
        send(blk.at[j, 1 - c], tpr.at[j], q_ss.at[j], q_rs.at[j], sibling)

    def scatter(j):
        take(tpr.at[j], q_rs.at[j])
        tsum[j] = total_of(blk[j, c], tpr[j]).astype(BF)
        for i, k in enumerate(CHIPS[j]):
            send(tsum.at[j, i], t1r.at[k % 8], t_ss.at[k % 8], t_rs.at[k % 8], at_z(k))

    def spread(j, part):
        for i in range(4):
            blk[j, i % 2, i // 2] = part[64 * i:64 * i + 64]
        for i, k in enumerate(CHIPS[j]):
            if k != 0:
                send(blk.at[j, c, i], tnear.at[j, i, 0], n_ss.at[j, i, 0], n_rs.at[j, i, 0], at_z(k))
            to = diagonal(k) if k != 0 else sibling
            send(blk.at[j, 1 - c, i], tnear.at[j, i, 1], n_ss.at[j, i, 1], n_rs.at[j, i, 1], to)

    def collect():
        spots = [(j, i, half) for j in (1, 0) for i in range(2) for half in range(2) if (j, i, half) != (0, 0, 0)]
        for k in range(3, 7):
            take(t1r.at[k], t_rs.at[k])
        for spot in spots:
            take(tnear.at[spot], n_rs.at[spot])
        mine = total_of(
            blk[0, c, 0], *[tnear[spot] for spot in spots], *[t1r[k] for k in range(3, 7)]
        ).astype(BF)
        own[...] = mine
        og[0, 0] = mine
        for kd, kc in CLUSTER:
            send(own, og.at[kd, kc], a_ss.at[kd, kc], a_rs.at[kd, kc], at_dc(kd, kc))
        for k in (1, 2, 3):
            send(own, gp.at[k], o_ss.at[k], o_rs.at[k], at_y(k))

    dkr[...] = backward(4, 4)
    for k in (1, 2, 3):
        send(dkr, gr.at[k], y_ss.at[k], y_rs.at[k], at_y(k))
    order = (2, 1, 3, 0)
    for i, r in enumerate(order):
        rows = pl.ds(pl.multiple_of(lax.rem(d + r, 4) * 1024, 1024), 1024)
        piece = dot(xrt[rows, :], dkr[...]).astype(BF)
        for b in range(16):
            pbuf[i, b % 2, b // 2] = piece[b * 64:(b + 1) * 64]
        send(pbuf.at[i, 1 - c], prcv.at[i], p_ss.at[i], p_rs.at[i], sibling)
    direct, summed = 2 - c, 1 + c
    out = forward(4)
    for u in range(16):
        op[:, u * HD:(u + 1) * HD] = out[u * 64:(u + 1) * 64]
    local.append(move(8, op, op_h))
    take(prcv.at[0], p_rs.at[0])
    x_s[0] = total_of(pbuf[0, c], prcv[0]).astype(BF)
    send(x_s.at[0], x_r.at[0], x_ss.at[0], x_rs.at[0], at_x(s))

    pair_up(3, backward(3, 5))
    take(prcv.at[direct], p_rs.at[direct])
    x_s[1] = total_of(pbuf[direct, c], prcv[direct]).astype(BF)
    send(x_s.at[1], x_r.at[1], x_ss.at[1], x_rs.at[1], at_x(-s))
    pair_up(2, backward(2, 5))
    scatter(3)
    spread(1, backward(1, 5))
    scatter(2)
    take(prcv.at[summed], p_rs.at[summed])
    take(x_r.at[0], x_rs.at[0])
    x_s[2] = total_of(pbuf[summed, c], prcv[summed], x_r[0]).astype(BF)
    send(x_s.at[2], x_r.at[2], x_ss.at[2], x_rs.at[2], at_x(s))
    spread(0, backward(0, 5))

    def grad_q_block(t):
        rows = slice(t * ROWS, (t + 1) * ROWS)
        grad_q = dot(ws[rows, 0:CH], kv_of(0)[:, 0:HD])
        for j in range(1, 5):
            grad_q = grad_q + dot(ws[rows, j * CH:(j + 1) * CH], kv_of(j)[:, 0:HD])
        grad_q = (grad_q * LN2).astype(BF)
        for u in range(4):
            gqr[:, (t * 4 + u) * HD:(t * 4 + u + 1) * HD] = grad_q[u * 256:(u + 1) * 256]

    grad_q_block(0)
    grad_q_block(1)
    grad_q_block(2)
    collect()
    grad_q_block(3)
    local.append(move(9, gqr, gqr_h))
    rows = slice(4 * ROWS, 5 * ROWS)
    grad_q = dot(ws[rows, 0:CH], kv_of(0)[:, 0:HD])
    for j in range(1, 4):
        grad_q = grad_q + dot(ws[rows, j * CH:(j + 1) * CH], kv_of(j)[:, 0:HD])
    grad_q = (grad_q * LN2).astype(BF)
    for u in range(16):
        gqp[:, u * HD:(u + 1) * HD] = grad_q[u * 64:(u + 1) * 64]
    local.append(move(10, gqp, gqp_h))

    for kd, kc in CLUSTER:
        take(xg.at[kd, kc], xg_rs.at[kd, kc])
    xgt[...] = xg[...].reshape(512, 512).T
    take(prcv.at[3], p_rs.at[3])
    take(x_r.at[1], x_rs.at[1])
    take(x_r.at[2], x_rs.at[2])
    z_f[...] = total_of(pbuf[3, c], prcv[3], x_r[1], x_r[2])
    for kd, kc in CLUSTER:
        take(og.at[kd, kc], a_rs.at[kd, kc])
    z_f[...] += dot(xgt[...], og[...].reshape(512, 256)).reshape(8, 64, 256)
    z_s[...] = z_f[...].astype(BF)
    for slot, block, to in ((2, 4, 2 * s), (0, 3, 1), (1, -3, -1), (3, 1, 1), (4, -1, -1)):
        send(z_s.at[zth(block)], z_r.at[slot], z_ss.at[slot], z_rs.at[slot], at_z(to))
    w_own = wv[pl.ds(pl.multiple_of(h * 1024, 1024), 1024), :]
    for k in (1, 2, 3):
        take(wr.at[k], w_rs.at[k])
        take(gr.at[k], y_rs.at[k])
    gxr[...] = (dot_nt(dkr[...], w_own) + dot_nt(gr[1], wr[1]) + dot_nt(gr[2], wr[2]) + dot_nt(gr[3], wr[3])).astype(BF)
    local.append(move(11, gxr, gxr_h))
    for slot in range(3):
        take(z_r.at[slot], z_rs.at[slot])
    z_m[0] = total_of(z_f[zth(2 * s)], z_r[c], z_r[2]).astype(BF)
    send(z_m.at[0], z_r.at[5], z_ss.at[5], z_rs.at[5], at_z(2 * s))
    z_m[1] = total_of(z_f[zth(-2 * s)], z_r[1 - c]).astype(BF)
    send(z_m.at[1], z_r.at[6], z_ss.at[6], z_rs.at[6], at_z(-2 * s))

    for k in (1, 2, 3):
        take(gp.at[k], o_rs.at[k])
    gxp[...] = (dot_nt(own[...], w_own) + dot_nt(gp[1], wr[1]) + dot_nt(gp[2], wr[2]) + dot_nt(gp[3], wr[3])).astype(BF)
    local.append(move(12, gxp, gxp_h))
    for copy in started[:-2]:
        copy.wait_send()
    for copy in local:
        copy.wait()
    for slot in (3, 4, 5, 6):
        take(z_r.at[slot], z_rs.at[slot])
    gw[...] = total_of(z_f[z], z_r[3], z_r[4], z_r[5], z_r[6])
    last = move(13, gw, gw_h)
    for copy in started[-2:]:
        copy.wait_send()
    last.wait()


def layer(length, xp, xr, w, qp, qr, dop, dor):
    dma = pltpu.SemaphoreType.DMA
    bf = lambda *shape: pltpu.VMEM(shape, BF)
    f32 = lambda *shape: pltpu.VMEM(shape, F32)
    block = (8, 64, 256)
    outs = [
        jax.ShapeDtypeStruct((64, 2048), BF), jax.ShapeDtypeStruct((256, 2048), BF),
        jax.ShapeDtypeStruct((64, 2048), BF), jax.ShapeDtypeStruct((256, 2048), BF),
        jax.ShapeDtypeStruct((64, 1024), BF), jax.ShapeDtypeStruct((256, 1024), BF),
        jax.ShapeDtypeStruct((64, 256), F32),
    ]
    return pl.pallas_call(
        layer_kernel,
        in_specs=[ANY] * 8,
        out_specs=[ANY] * 7,
        out_shape=outs,
        scratch_shapes=[
            pltpu.SMEM((1, 1), jnp.int32),
            bf(64, 4096), bf(256, 4096), bf(4096, 256), bf(64, 2048), bf(256, 2048), bf(64, 2048), bf(256, 2048),
            bf(64, 2048), bf(256, 2048), bf(64, 2048), bf(256, 2048), bf(64, 1024), bf(256, 1024), f32(64, 256),
            bf(8, 2, 64, 256), bf(256, 256), bf(4, 256, 256), bf(256, 1280), bf(4096, 256), bf(4, 2, 64, 512), bf(4, 2, 64, 512),
            bf(512, 512),            bf(4, 1024, 256),
            bf(5120, 1280), bf(5120, HD), bf(5120, HD), bf(HD, 5120), bf(HD, 5120),
            f32(5120, 128), f32(256, 256),
            bf(4, 2, 2, 64, 256), bf(4, 2, 64, 256), bf(4, 2, 64, 256), bf(8, 64, 256), bf(2, 2, 2, 64, 256), bf(64, 256),
            bf(4, 2, 64, 256), bf(4, 64, 256),
            bf(4, 256, 256), bf(256, 256),
            bf(4, 2, *block), bf(4, *block), bf(3, *block), bf(3, *block), f32(*block), bf(*block), bf(*block), bf(2, 64, 256),
            dma((15,)), dma((8,)), dma((8,)), dma((8,)), dma((8,)), dma((4,)), dma((4,)), dma((4, 2)), dma((4, 2)),
            dma((8,)), dma((8,)), dma((4, 2)), dma((4, 2)),
            dma((4,)), dma((4,)), dma((4,)), dma((4,)), dma((4,)), dma((4,)), dma((3,)), dma((3,)),
            dma((8,)), dma((8,)), dma((4,)), dma((4,)), dma((2, 2, 2)), dma((2, 2, 2)),
        ],
        compiler_params=pltpu.CompilerParams(
            collective_id=0, has_side_effects=True, vmem_limit_bytes=60 << 20
        ),
        cost_estimate=pl.CostEstimate(
            flops=22_000_000_000, bytes_accessed=12 << 20, transcendentals=6_500_000
        ),
        name="layer",
    )(length, xp, xr, w, qp, qr, dop, dor)


def finish_kernel(*refs):
    n = len(refs[:-2]) // 3
    came, went = refs[-2:]
    ins, outs, held = refs[:n], refs[n:2 * n], refs[2 * n:3 * n]
    reads = [pltpu.make_async_copy(ins[i], held[i], came.at[i]) for i in range(n)]
    writes = [pltpu.make_async_copy(held[i], outs[i], went.at[i]) for i in range(n)]
    for copy in reads:
        copy.start()
    for i in range(n):
        reads[i].wait()
        writes[i].start()
    for copy in writes:
        copy.wait()


def finish(arrays):
    n = len(arrays)
    return pl.pallas_call(
        finish_kernel,
        in_specs=[ANY] * n,
        out_specs=[ANY] * n,
        out_shape=[jax.ShapeDtypeStruct(a.shape, a.dtype) for a in arrays],
        scratch_shapes=[pltpu.VMEM(a.shape, a.dtype) for a in arrays] + [pltpu.SemaphoreType.DMA((n,))] * 2,
        name="finish",
    )(*arrays)


def body(x_prompt, x_resp, w_kv, q_prompt, q_resp, do_prompt, do_resp, resp_len):
    arrays = layer(
        resp_len, x_prompt[0], x_resp[0], w_kv, q_prompt[0], q_resp[0], do_prompt[0], do_resp[0]
    )
    op, out_r, gqp, gqr, gxp, gxr, gw = finish(arrays)
    return op[None], out_r[None], gqp[None], gqr[None], gxp[None], gxr[None], gw


def solution(mesh):
    return jax.shard_map(
        body,
        mesh=mesh,
        in_specs=(
            P("dp", "pool", None),
            P("dp", "pool", None),
            P(None, "head"),
            P("dp", "pool", "head"),
            P("dp", "pool", "head"),
            P("dp", "pool", "head"),
            P("dp", "pool", "head"),
            P("dp", "pool"),
        ),
        out_specs=(
            P("dp", "pool", "head"),
            P("dp", "pool", "head"),
            P("dp", "pool", "head"),
            P("dp", "pool", "head"),
            P("dp", "pool", "head"),
            P("dp", "pool", "head"),
            P(("dp", "pool"), "head"),
        ),
        check_vma=False,
    )
```
